32 devices in a mesh: fsdp: 16 (over z, y, core), rep: 2 (over x), dp: 1.
Axes of the slice: x: 2, y: 2, z: 4, core: 2. Of those that a mesh axis runs over, the one named last changes fastest.
Arguments:
- trainer_gate: bfloat16 [8192, 1, 4096], P('fsdp', 'dp'), may hold values from -0.0625 to 0.0625
- trainer_up: bfloat16 [8192, 1, 4096], P('fsdp', 'dp'), may hold values from -0.0625 to 0.0625
- owner_map: int32 [64], replicated, may hold values from 0 to 63, each once
- sketch_seeds: int32 [8192], replicated, may hold values from 0 to 1
- probes: bfloat16 [2, 16, 128, 8192], P('rep', 'fsdp'), may hold values from -6 to 6
Outputs:
- digest: float32 [2, 64, 1, 4096], P(None, None, 'dp', 'fsdp')
- hidden: bfloat16 [2, 16, 128, 1, 256], P('rep', 'fsdp', None, 'dp')
The draws below stay inside these ranges and needn't reach their ends.
Inputs may be any that keep to these rules, and one draw needn't show every extreme that they name: owner_map is a permutation: every true row block is held at exactly one trainer position.
All inputs are finite; a program needn't handle non-finite values.
Results may differ from the reference program's by a relative error of at most 0.01.
Values may be sent and summed in bfloat16 or wider, within the bound.
A program may use at most 64 MiB of HBM per device.

```python
import jax
import jax.numpy as jnp
from jax import lax

D = 8192
FDP = 4096
PROBE = 128
BLOCKS = 64
N_FSDP = 16
N_REP = 2
N_DP = 1


def with_ends(array, key, low, high):
    shape = array.shape
    place = [jax.random.randint(jax.random.fold_in(key, axis), (), 0, shape[axis]) for axis in range(len(shape))]
    array = array.at[tuple(place)].set(low)
    longest = shape.index(max(shape))
    place[longest] = (place[longest] + 1) % shape[longest]
    return array.at[tuple(place)].set(high)


def steps_of(rng, extent, cuts, low, high):
    loudness, own = 1.0, jax.random.fold_in(rng, 6)
    for position, blocks in cuts:
        steps = jnp.exp(jax.random.uniform(jax.random.fold_in(own, position), (blocks,), jnp.float32, low / len(cuts), high / len(cuts)))
        loudness = loudness * jnp.repeat(steps, extent[position] // blocks).reshape([-1 if axis == position else 1 for axis in range(len(extent))])
    return loudness


def bell_draw(rng, dims, scale, reach, cuts=(), held_as=jnp.bfloat16):
    drawn = jax.random.normal(rng, dims, jnp.float32) * scale
    if len(cuts) > 0:
        drawn = steps_of(rng, dims, cuts, -0.22, 0.18) * drawn
    return jnp.clip(drawn, min=-reach, max=reach).astype(held_as)


def setup_inputs(seed: int = 0) -> dict:
    keys = jax.random.split(jax.random.key(seed), 6)
    return {
        "trainer_gate": bell_draw(keys[0], (D, N_DP, FDP), D ** -0.5, 0.0625, ((0, 16),)),
        "trainer_up": bell_draw(keys[1], (D, N_DP, FDP), D ** -0.5, 0.0625, ((0, 16),)),
        "owner_map": jax.random.permutation(keys[2], BLOCKS).astype(jnp.int32),
        "sketch_seeds": with_ends(jax.random.randint(keys[3], (D,), 0, 2), jax.random.fold_in(keys[3], 1), 0, 1).astype(jnp.int32),
        "probes": bell_draw(keys[4], (N_REP, N_FSDP, PROBE, D), 1.0, 6.0, ((0, 2), (1, 16))),
    }


def restore(matrix, inverse):
    blocks_all = D // 128
    pieces = matrix.reshape(blocks_all, 128 * N_DP * FDP)
    return pieces[inverse].reshape(D, N_DP, FDP)

def sketch(matrix, signs):
    blocks_all = D // 128
    viewed = matrix.reshape(blocks_all, 128, N_DP, FDP).astype(jnp.float32)
    return 8.0 * lax.optimization_barrier(jnp.sum(signs * viewed, axis=1))

def reference(trainer_gate, trainer_up, owner_map, sketch_seeds, probes):
    ranks = min(16, N_FSDP)
    subs = N_FSDP // ranks
    width = FDP // ranks
    inverse = jnp.argsort(owner_map).astype(jnp.int32)
    gate_true = restore(trainer_gate, inverse)
    up_true = restore(trainer_up, inverse)
    signs = (1 - 2 * sketch_seeds).astype(jnp.float32).reshape(D // 128, 128, 1, 1)
    digest = jnp.stack([sketch(gate_true, signs), sketch(up_true, signs)])

    def one_device(member):
        rows = lax.dynamic_index_in_dim(probes, member, 1, keepdims=False)
        wide = rows.reshape(N_REP * PROBE, D).astype(jnp.float32)
        meansq = lax.optimization_barrier(jnp.mean(wide * wide, axis=-1, keepdims=True))
        normed = (wide / jnp.sqrt(meansq + 1e-05)).astype(jnp.bfloat16)
        start = member // subs * width
        gate_cols = lax.dynamic_slice_in_dim(gate_true, start, width, 2).reshape(D, N_DP * width)
        up_cols = lax.dynamic_slice_in_dim(up_true, start, width, 2).reshape(D, N_DP * width)
        gate_out = jnp.dot(normed, gate_cols, preferred_element_type=jnp.float32)
        up_out = jnp.dot(normed, up_cols, preferred_element_type=jnp.float32)
        result = (jax.nn.silu(gate_out) * up_out).astype(jnp.bfloat16)
        return result.reshape(N_REP, PROBE, N_DP, width)
    stacked = lax.map(one_device, jnp.arange(N_FSDP, dtype=jnp.int32))
    return (digest, jnp.transpose(stacked, (1, 0, 2, 3, 4)))
```

```python
import functools

import jax
import jax.numpy as jnp
from jax import lax
from jax.experimental import pallas as pl
from jax.experimental.pallas import tpu as pltpu
from jax.sharding import PartitionSpec as P

MESH = pl.DeviceIdType.MESH
LANES = 128


def kernel(
    count, group, subgroups, width, blocks,
    probes_hbm, gate_hbm, up_hbm, owner_hbm, seeds_hbm,
    digest_ref, hidden_ref,
    owner_ref, seeds_ref, x, gate, up, stage, got, part, part_in, total, plane_out, plane_in, dig_out, dig_in,
    x_load, load_sem, x_send, x_recv, p_send, p_recv, z_send, z_recv, d_send, d_recv,
):
    planes = count // group
    rows = x.shape[1]
    local_rows = gate.shape[0]
    nb = local_rows // LANES
    ranks = dig_out.shape[0]
    dig_rows = dig_out.shape[1]
    me = lax.axis_index("fsdp")
    plane, spot = me // group, me % group

    def peer(index):
        return {"fsdp": index}

    def remote(src, dst, send, recv, index):
        return pltpu.make_async_remote_copy(
            src_ref=src, dst_ref=dst, send_sem=send, recv_sem=recv,
            device_id=peer(index), device_id_type=MESH,
        )

    load_owner = pltpu.make_async_copy(owner_hbm, owner_ref, load_sem.at[2])
    load_seeds = pltpu.make_async_copy(seeds_hbm, seeds_ref, load_sem.at[3])
    load_owner.start()

    def load_x(block):
        columns = pl.ds(pl.multiple_of(block * LANES, LANES), LANES)
        return pltpu.make_async_copy(probes_hbm.at[:, columns], x.at[block], x_load.at[block])

    def start_x(block, carry):
        load_x(block).start()
        return carry

    def wait_x(block, carry):
        load_x(block).wait()
        return carry

    lax.fori_loop(0, blocks, start_x, 0)
    load_gate = pltpu.make_async_copy(gate_hbm, gate, load_sem.at[0])
    load_up = pltpu.make_async_copy(up_hbm, up, load_sem.at[1])
    load_gate.start()
    load_up.start()
    load_seeds.start()

    barrier = pltpu.get_barrier_semaphore()

    def greet(step, carry):
        pl.semaphore_signal(
            barrier, inc=1, device_id=peer((me + step) % count), device_id_type=MESH
        )
        return carry

    lax.fori_loop(1, count, greet, 0)
    load_owner.wait()
    lax.fori_loop(0, blocks, wait_x, 0)

    def pick(target, into):
        for i in range(nb):
            block = owner_ref[target * nb + i]
            into[target, :, i * LANES : (i + 1) * LANES] = x[block]

    phases = sorted(range(1, planes), key=lambda k: -min(k, planes - k))

    def x_copy(target):
        return remote(stage.at[target], got.at[me], x_send.at[target], x_recv.at[me], target)

    def x_arrival(source):
        return remote(stage.at[source], got.at[source], x_send.at[source], x_recv.at[source], source)

    pl.semaphore_wait(barrier, count - 1)
    def send(k, j):
        target = ((plane + k) % planes) * group + (spot + j) % group
        pick(target, stage)
        x_copy(target).start()

    def send_phase(k, last):
        def one(j, carry):
            send(k, j)
            return carry

        lax.fori_loop(1, last, one, 0)

    send_phase(phases[0], group + 1)
    send_phase(0, group)
    pick(me, got)

    def squares(block, acc):
        wide = x[block].astype(jnp.float32)
        return acc + wide * wide

    acc = lax.fori_loop(0, blocks, squares, jnp.zeros((rows, LANES), jnp.float32))
    meansq = jnp.sum(acc, axis=1, keepdims=True) / (blocks * LANES)
    scale = 1.0 / jnp.sqrt(meansq + 1e-05)

    load_seeds.wait()
    row_id = lax.broadcasted_iota(jnp.int32, (16, LANES), 0)
    for_gate, for_up = [], []
    for i in range(nb):
        held = lax.broadcasted_iota(jnp.int32, seeds_ref.shape, 0) == owner_ref[me * nb + i]
        seeds = jnp.sum(jnp.where(held, seeds_ref[...], 0), axis=0, keepdims=True)
        signs = jnp.broadcast_to(8 * (1 - 2 * seeds), (16, LANES)).astype(jnp.float32)
        for_gate.append(jnp.where(row_id == i, signs, 0.0))
        for_up.append(jnp.where(row_id == nb + i, signs, 0.0))
    for_gate = jnp.concatenate(for_gate, axis=1).astype(jnp.bfloat16)
    for_up = jnp.concatenate(for_up, axis=1).astype(jnp.bfloat16)
    load_gate.wait()
    load_up.wait()

    def columns_of(t):
        return pl.ds(pl.multiple_of(t * width, width), width)

    def sketch(t, carry):
        both = jnp.dot(for_gate, gate[:, columns_of(t)], preferred_element_type=jnp.float32)
        both += jnp.dot(for_up, up[:, columns_of(t)], preferred_element_type=jnp.float32)
        dig_out[t] = both[:dig_rows]
        return carry

    lax.fori_loop(0, ranks, sketch, 0)
    dig_in[me] = dig_out[me // subgroups]

    def d_copy(target):
        return remote(
            dig_out.at[target // subgroups], dig_in.at[me], d_send.at[target], d_recv.at[me], target
        )

    def d_arrival(source):
        return remote(
            dig_out.at[source // subgroups], dig_in.at[source], d_send.at[source],
            d_recv.at[source], source,
        )

    def send_digest(step, carry):
        d_copy((me + step) % count).start()
        return carry

    lax.fori_loop(1, count, send_digest, 0)

    def product(source):
        rows_of = got[source]
        columns = columns_of(source // subgroups)
        return (
            jnp.dot(rows_of, gate[:, columns], preferred_element_type=jnp.float32),
            jnp.dot(rows_of, up[:, columns], preferred_element_type=jnp.float32),
        )

    def p_copy(source_plane, spot_to):
        return remote(
            part.at[source_plane * group + spot_to],
            part_in.at[source_plane * group + spot],
            p_send.at[source_plane * group + spot_to],
            p_recv.at[source_plane * group + spot],
            plane * group + spot_to,
        )

    def p_arrival(source_plane, spot_from):
        index = source_plane * group + spot_from
        return remote(
            part.at[index], part_in.at[index], p_send.at[index], p_recv.at[index],
            plane * group + spot_from,
        )

    def z_copy(source_plane):
        return remote(
            plane_out.at[source_plane], plane_in.at[plane], z_send.at[source_plane],
            z_recv.at[plane], source_plane * group + spot,
        )

    def z_arrival(from_plane):
        return remote(
            plane_out.at[from_plane], plane_in.at[from_plane], z_send.at[from_plane],
            z_recv.at[from_plane], from_plane * group + spot,
        )

    def multiply(source_plane, k, following):
        def others(j, carry):
            spot_from = (spot + group - j) % group
            source = source_plane * group + spot_from
            x_arrival(source).wait_recv()
            if following is not None:
                send(following, j)
            a, b = product(source)
            part[source, :, :width] = a.astype(jnp.bfloat16)
            part[source, :, width:] = b.astype(jnp.bfloat16)
            p_copy(source_plane, spot_from).start()
            return carry

        lax.fori_loop(1, group, others, 0)
        source = source_plane * group + spot
        if k != 0:
            x_arrival(source).wait_recv()
            if following is not None:
                send(following, group)
        a, b = product(source)
        total[source_plane, :, :width] = a
        total[source_plane, :, width:] = b

    def reduce(source_plane):
        def add(j, carry):
            spot_from = (spot + group - j) % group
            p_arrival(source_plane, spot_from).wait_recv()
            total[source_plane] += part_in[source_plane * group + spot_from].astype(jnp.float32)
            return carry

        lax.fori_loop(1, group, add, 0)

    def reduce_away(source_plane):
        reduce(source_plane)
        plane_out[source_plane] = total[source_plane].astype(jnp.bfloat16)
        z_copy(source_plane).start()

    multiply(plane, 0, None)
    for p, k in enumerate(phases):
        source_plane = (plane + planes - k) % planes
        multiply(source_plane, k, phases[p + 1] if p + 1 < len(phases) else None)
        if p == 0:
            reduce(plane)
        else:
            reduce_away((plane + planes - phases[p - 1]) % planes)
    reduce_away((plane + planes - phases[-1]) % planes)

    def wait_digest(step, carry):
        d_arrival((me + step) % count).wait_recv()
        return carry

    lax.fori_loop(1, count, wait_digest, 0)
    span = count * dig_rows
    column = lax.broadcasted_iota(jnp.int32, (8, span), 1)
    inner = column % dig_rows
    place = jnp.where(inner < 2 * nb, (column // dig_rows) * nb + inner % nb, -1)
    owners = jnp.full((8, span), -1, jnp.int32)
    for j in range(blocks):
        owners = jnp.where(place == j, owner_ref[j], owners)
    owners = owners + jnp.where(inner >= nb, blocks, 0)
    owners = jnp.where(inner < 2 * nb, owners, -1)
    wanted = lax.broadcasted_iota(jnp.int32, (2 * blocks, span), 0)
    chosen = jnp.where(jnp.broadcast_to(owners[:1], (2 * blocks, span)) == wanted, 1.0, 0.0)
    digest_ref[...] = jnp.dot(
        chosen, dig_in[...].reshape(span, width),
        precision=lax.Precision.HIGHEST, preferred_element_type=jnp.float32,
    )

    def gather_planes(step, carry):
        from_plane = (plane + planes - step) % planes
        z_arrival(from_plane).wait_recv()
        total[plane] += plane_in[from_plane].astype(jnp.float32)
        return carry

    for k in phases:
        gather_planes(k, 0)
    gate_sum = total[plane, :, :width] * scale
    up_sum = total[plane, :, width:] * scale
    hidden_ref[...] = (gate_sum / (1.0 + jnp.exp(-gate_sum)) * up_sum).astype(jnp.bfloat16)

    def drain(step, carry):
        target = (me + step) % count
        x_copy(target).wait_send()
        d_copy(target).wait_send()
        return carry

    lax.fori_loop(1, count, drain, 0)

    def drain_plane(source_plane, carry):
        def drain_spot(j, inner_carry):
            p_copy(source_plane, (spot + group - j) % group).wait_send()
            return inner_carry

        return lax.fori_loop(1, group, drain_spot, carry)

    lax.fori_loop(0, planes, drain_plane, 0)

    def drain_away(step, carry):
        z_copy((plane + step) % planes).wait_send()
        return carry

    lax.fori_loop(1, planes, drain_away, 0)


def on_device(trainer_gate, trainer_up, owner_map, sketch_seeds, probes):
    local_rows, _, slice_width = trainer_gate.shape
    count = lax.axis_size("fsdp")
    ranks = min(16, count)
    subgroups = count // ranks
    width = slice_width // ranks
    narrow = width // subgroups
    group = 4
    planes = count // group
    total_rows = local_rows * count
    blocks = total_rows // LANES
    nb = local_rows // LANES
    dig_rows = -(-2 * nb // 8) * 8
    rows = probes.shape[2]
    bf16, f32 = jnp.bfloat16, jnp.float32
    dma = pltpu.SemaphoreType.DMA
    digest, hidden = pl.pallas_call(
        functools.partial(kernel, count, group, subgroups, width, blocks),
        out_shape=(
            jax.ShapeDtypeStruct((2 * blocks, width), f32),
            jax.ShapeDtypeStruct((rows, width), bf16),
        ),
        in_specs=[pl.BlockSpec(memory_space=pl.ANY)] * 5,
        out_specs=[pl.BlockSpec(memory_space=pltpu.VMEM)] * 2,
        scratch_shapes=[
            pltpu.SMEM((blocks,), jnp.int32),
            pltpu.VMEM((blocks, LANES), jnp.int32),
            pltpu.VMEM((blocks, rows, LANES), bf16),
            pltpu.VMEM((local_rows, slice_width), bf16),
            pltpu.VMEM((local_rows, slice_width), bf16),
            pltpu.VMEM((count, rows, local_rows), bf16),
            pltpu.VMEM((count, rows, local_rows), bf16),
            pltpu.VMEM((count, rows, 2 * width), bf16),
            pltpu.VMEM((count, rows, 2 * width), bf16),
            pltpu.VMEM((planes, rows, 2 * width), f32),
            pltpu.VMEM((planes, rows, 2 * width), bf16),
            pltpu.VMEM((planes, rows, 2 * width), bf16),
            pltpu.VMEM((ranks, dig_rows, width), f32),
            pltpu.VMEM((count, dig_rows, width), f32),
            dma((blocks,)), dma((4,)),
            dma((count,)), dma((count,)),
            dma((count,)), dma((count,)),
            dma((planes,)), dma((planes,)),
            dma((count,)), dma((count,)),
        ],
        compiler_params=pltpu.CompilerParams(
            collective_id=0, has_side_effects=True, vmem_limit_bytes=60 * 2**20
        ),
    )(
        probes.reshape(rows, total_rows),
        trainer_gate.reshape(local_rows, slice_width),
        trainer_up.reshape(local_rows, slice_width),
        owner_map,
        sketch_seeds.reshape(blocks, LANES),
    )
    if subgroups > 1:
        member = lax.axis_index("fsdp")
        digest = lax.dynamic_slice_in_dim(digest, (member % subgroups) * narrow, narrow, 1)
    return (
        digest.reshape(2, blocks, 1, narrow),
        hidden.reshape(1, 1, rows, 1, width),
    )


def solution(mesh):
    placed = (P("fsdp", "dp", None), P("fsdp", "dp", None), P(), P(), P("rep", "fsdp", None, None))
    return jax.shard_map(
        on_device,
        mesh=mesh,
        in_specs=placed,
        out_specs=(P(None, None, "dp", "fsdp"), P("rep", "fsdp", None, "dp", None)),
        check_vma=False,
    )
```

```python
import functools

import jax
import jax.numpy as jnp
from jax import lax
from jax.experimental import pallas as pl
from jax.experimental.pallas import tpu as pltpu
from jax.sharding import PartitionSpec as P

MESH = pl.DeviceIdType.MESH
LANES = 128


def kernel(
    count, group, subgroups, width, blocks,
    probes_hbm, gate_hbm, up_hbm, owner_hbm, seeds_hbm,
    digest_ref, hidden_ref,
    owner_ref, seeds_ref, x, gate, up, stage, got, part, part_in, total, plane_out, plane_in, dig_out, dig_in,
    x_load, load_sem, x_send, x_recv, p_send, p_recv, z_send, z_recv, d_send, d_recv,
):
    planes = count // group
    rows = x.shape[1]
    local_rows = gate.shape[0]
    nb = local_rows // LANES
    ranks = dig_out.shape[0]
    dig_rows = dig_out.shape[1]
    me = lax.axis_index("fsdp")
    plane, spot = me // group, me % group

    def peer(index):
        return {"fsdp": index}

    def remote(src, dst, send, recv, index):
        return pltpu.make_async_remote_copy(
            src_ref=src, dst_ref=dst, send_sem=send, recv_sem=recv,
            device_id=peer(index), device_id_type=MESH,
        )

    load_owner = pltpu.make_async_copy(owner_hbm, owner_ref, load_sem.at[2])
    load_seeds = pltpu.make_async_copy(seeds_hbm, seeds_ref, load_sem.at[3])
    load_owner.start()

    def load_x(block):
        columns = pl.ds(pl.multiple_of(block * LANES, LANES), LANES)
        return pltpu.make_async_copy(probes_hbm.at[:, columns], x.at[block], x_load.at[block])

    def start_x(block, carry):
        load_x(block).start()
        return carry

    def wait_x(block, carry):
        load_x(block).wait()
        return carry

    lax.fori_loop(0, blocks, start_x, 0)
    load_gate = pltpu.make_async_copy(gate_hbm, gate, load_sem.at[0])
    load_up = pltpu.make_async_copy(up_hbm, up, load_sem.at[1])
    load_gate.start()
    load_up.start()
    load_seeds.start()

    barrier = pltpu.get_barrier_semaphore()

    def greet(step, carry):
        pl.semaphore_signal(
            barrier, inc=1, device_id=peer((me + step) % count), device_id_type=MESH
        )
        return carry

    lax.fori_loop(1, count, greet, 0)
    load_owner.wait()
    lax.fori_loop(0, blocks, wait_x, 0)

    def pick(target, into):
        for i in range(nb):
            block = owner_ref[target * nb + i]
            into[target, :, i * LANES : (i + 1) * LANES] = x[block]


    def x_copy(target):
        return remote(stage.at[target], got.at[me], x_send.at[target], x_recv.at[me], target)

    def x_arrival(source):
        return remote(stage.at[source], got.at[source], x_send.at[source], x_recv.at[source], source)

    pl.semaphore_wait(barrier, count - 1)
    def partner(m):
        other = plane * 0
        for bit in range((planes - 1).bit_length()):
            digit = (plane // 2**bit) % 2
            other = other + 2**bit * (1 - digit if (m >> bit) & 1 else digit)
        return other

    def send(m, j):
        target = partner(m) * group + (spot + j) % group
        pick(target, stage)
        x_copy(target).start()

    def send_phase(m, last):
        def one(j, carry):
            send(m, j)
            return carry

        lax.fori_loop(1, last, one, 0)

    send_phase(2, group + 1)
    send_phase(0, group)
    send_phase(1, group + 1)
    pick(me, got)

    def squares(block, acc):
        wide = x[block].astype(jnp.float32)
        return acc + wide * wide

    acc = lax.fori_loop(0, blocks, squares, jnp.zeros((rows, LANES), jnp.float32))
    meansq = jnp.sum(acc, axis=1, keepdims=True) / (blocks * LANES)
    scale = 1.0 / jnp.sqrt(meansq + 1e-05)

    load_seeds.wait()
    row_id = lax.broadcasted_iota(jnp.int32, (16, LANES), 0)
    for_gate, for_up = [], []
    for i in range(nb):
        held = lax.broadcasted_iota(jnp.int32, seeds_ref.shape, 0) == owner_ref[me * nb + i]
        seeds = jnp.sum(jnp.where(held, seeds_ref[...], 0), axis=0, keepdims=True)
        signs = jnp.broadcast_to(8 * (1 - 2 * seeds), (16, LANES)).astype(jnp.float32)
        for_gate.append(jnp.where(row_id == i, signs, 0.0))
        for_up.append(jnp.where(row_id == nb + i, signs, 0.0))
    for_gate = jnp.concatenate(for_gate, axis=1).astype(jnp.bfloat16)
    for_up = jnp.concatenate(for_up, axis=1).astype(jnp.bfloat16)
    load_gate.wait()
    load_up.wait()

    def columns_of(t):
        return pl.ds(pl.multiple_of(t * width, width), width)

    def sketch(t, carry):
        both = jnp.dot(for_gate, gate[:, columns_of(t)], preferred_element_type=jnp.float32)
        both += jnp.dot(for_up, up[:, columns_of(t)], preferred_element_type=jnp.float32)
        dig_out[t] = both[:dig_rows]
        return carry

    lax.fori_loop(0, ranks, sketch, 0)
    dig_in[me] = dig_out[me // subgroups]

    def d_copy(target):
        return remote(
            dig_out.at[target // subgroups], dig_in.at[me], d_send.at[target], d_recv.at[me], target
        )

    def d_arrival(source):
        return remote(
            dig_out.at[source // subgroups], dig_in.at[source], d_send.at[source],
            d_recv.at[source], source,
        )

    def send_digest(step, carry):
        d_copy((me + step) % count).start()
        return carry

    lax.fori_loop(1, count, send_digest, 0)

    def product(source):
        rows_of = got[source]
        columns = columns_of(source // subgroups)
        return (
            jnp.dot(rows_of, gate[:, columns], preferred_element_type=jnp.float32),
            jnp.dot(rows_of, up[:, columns], preferred_element_type=jnp.float32),
        )

    def p_copy(source_plane, spot_to):
        return remote(
            part.at[source_plane * group + spot_to],
            part_in.at[source_plane * group + spot],
            p_send.at[source_plane * group + spot_to],
            p_recv.at[source_plane * group + spot],
            plane * group + spot_to,
        )

    def p_arrival(source_plane, spot_from):
        index = source_plane * group + spot_from
        return remote(
            part.at[index], part_in.at[index], p_send.at[index], p_recv.at[index],
            plane * group + spot_from,
        )

    def z_copy(m):
        return remote(
            plane_out.at[m], plane_in.at[m], z_send.at[m], z_recv.at[m],
            partner(m if m % 2 else 1) * group + spot,
        )

    def multiply(m, following):
        source_plane = partner(m)

        def others(j, carry):
            spot_from = (spot + group - j) % group
            source = source_plane * group + spot_from
            x_arrival(source).wait_recv()
            if following is not None:
                send(following, j)
            a, b = product(source)
            part[source, :, :width] = a.astype(jnp.bfloat16)
            part[source, :, width:] = b.astype(jnp.bfloat16)
            p_copy(source_plane, spot_from).start()
            return carry

        lax.fori_loop(1, group, others, 0)
        source = source_plane * group + spot
        if m != 0:
            x_arrival(source).wait_recv()
            if following is not None:
                send(following, group)
        a, b = product(source)
        total[m, :, :width] = a
        total[m, :, width:] = b

    def reduce(m):
        source_plane = partner(m)

        def add(j, carry):
            spot_from = (spot + group - j) % group
            p_arrival(source_plane, spot_from).wait_recv()
            total[m] += part_in[source_plane * group + spot_from].astype(jnp.float32)
            return carry

        lax.fori_loop(1, group, add, 0)
        if m > 2 and m % 2:
            add_plane(m, m - 1)
        if m > 0:
            plane_out[m] = total[m].astype(jnp.bfloat16)
            z_copy(m).start()

    def add_plane(m, arrived):
        z_copy(arrived).wait_recv()
        total[m] += plane_in[arrived].astype(jnp.float32)

    steps = [0, 2, 1] + list(range(3, planes))
    before = None
    for m in steps:
        following = m + 1 if m >= 2 and m + 1 < planes else None
        multiply(m, following)
        if before is not None:
            reduce(before)
        before = m
    reduce(before)

    def wait_digest(step, carry):
        d_arrival((me + step) % count).wait_recv()
        return carry

    lax.fori_loop(1, count, wait_digest, 0)
    span = count * dig_rows
    column = lax.broadcasted_iota(jnp.int32, (8, span), 1)
    inner = column % dig_rows
    place = jnp.where(inner < 2 * nb, (column // dig_rows) * nb + inner % nb, -1)
    owners = jnp.full((8, span), -1, jnp.int32)
    for j in range(blocks):
        owners = jnp.where(place == j, owner_ref[j], owners)
    owners = owners + jnp.where(inner >= nb, blocks, 0)
    owners = jnp.where(inner < 2 * nb, owners, -1)
    wanted = lax.broadcasted_iota(jnp.int32, (2 * blocks, span), 0)
    chosen = jnp.where(jnp.broadcast_to(owners[:1], (2 * blocks, span)) == wanted, 1.0, 0.0)
    digest_ref[...] = jnp.dot(
        chosen, dig_in[...].reshape(span, width),
        precision=lax.Precision.HIGHEST, preferred_element_type=jnp.float32,
    )

    for m in range(1, planes, 2):
        add_plane(0, m)
    gate_sum = total[0, :, :width] * scale
    up_sum = total[0, :, width:] * scale
    hidden_ref[...] = (gate_sum / (1.0 + jnp.exp(-gate_sum)) * up_sum).astype(jnp.bfloat16)

    def drain(step, carry):
        target = (me + step) % count
        x_copy(target).wait_send()
        d_copy(target).wait_send()
        return carry

    lax.fori_loop(1, count, drain, 0)

    def drain_plane(source_plane, carry):
        def drain_spot(j, inner_carry):
            p_copy(source_plane, (spot + group - j) % group).wait_send()
            return inner_carry

        return lax.fori_loop(1, group, drain_spot, carry)

    lax.fori_loop(0, planes, drain_plane, 0)

    for m in range(1, planes):
        z_copy(m).wait_send()


def on_device(trainer_gate, trainer_up, owner_map, sketch_seeds, probes):
    local_rows, _, slice_width = trainer_gate.shape
    count = lax.axis_size("fsdp")
    ranks = min(16, count)
    subgroups = count // ranks
    width = slice_width // ranks
    narrow = width // subgroups
    group = 4
    planes = count // group
    total_rows = local_rows * count
    blocks = total_rows // LANES
    nb = local_rows // LANES
    dig_rows = -(-2 * nb // 8) * 8
    rows = probes.shape[2]
    bf16, f32 = jnp.bfloat16, jnp.float32
    dma = pltpu.SemaphoreType.DMA
    digest, hidden = pl.pallas_call(
        functools.partial(kernel, count, group, subgroups, width, blocks),
        out_shape=(
            jax.ShapeDtypeStruct((2 * blocks, width), f32),
            jax.ShapeDtypeStruct((rows, width), bf16),
        ),
        in_specs=[pl.BlockSpec(memory_space=pl.ANY)] * 5,
        out_specs=[pl.BlockSpec(memory_space=pltpu.VMEM)] * 2,
        scratch_shapes=[
            pltpu.SMEM((blocks,), jnp.int32),
            pltpu.VMEM((blocks, LANES), jnp.int32),
            pltpu.VMEM((blocks, rows, LANES), bf16),
            pltpu.VMEM((local_rows, slice_width), bf16),
            pltpu.VMEM((local_rows, slice_width), bf16),
            pltpu.VMEM((count, rows, local_rows), bf16),
            pltpu.VMEM((count, rows, local_rows), bf16),
            pltpu.VMEM((count, rows, 2 * width), bf16),
            pltpu.VMEM((count, rows, 2 * width), bf16),
            pltpu.VMEM((planes, rows, 2 * width), f32),
            pltpu.VMEM((planes, rows, 2 * width), bf16),
            pltpu.VMEM((planes, rows, 2 * width), bf16),
            pltpu.VMEM((ranks, dig_rows, width), f32),
            pltpu.VMEM((count, dig_rows, width), f32),
            dma((blocks,)), dma((4,)),
            dma((count,)), dma((count,)),
            dma((count,)), dma((count,)),
            dma((planes,)), dma((planes,)),
            dma((count,)), dma((count,)),
        ],
        compiler_params=pltpu.CompilerParams(
            collective_id=0, has_side_effects=True, vmem_limit_bytes=60 * 2**20
        ),
    )(
        probes.reshape(rows, total_rows),
        trainer_gate.reshape(local_rows, slice_width),
        trainer_up.reshape(local_rows, slice_width),
        owner_map,
        sketch_seeds.reshape(blocks, LANES),
    )
    if subgroups > 1:
        member = lax.axis_index("fsdp")
        digest = lax.dynamic_slice_in_dim(digest, (member % subgroups) * narrow, narrow, 1)
    return (
        digest.reshape(2, blocks, 1, narrow),
        hidden.reshape(1, 1, rows, 1, width),
    )


def solution(mesh):
    placed = (P("fsdp", "dp", None), P("fsdp", "dp", None), P(), P(), P("rep", "fsdp", None, None))
    return jax.shard_map(
        on_device,
        mesh=mesh,
        in_specs=placed,
        out_specs=(P(None, None, "dp", "fsdp"), P("rep", "fsdp", None, "dp", None)),
        check_vma=False,
    )
```

```python
import functools

import jax
import jax.numpy as jnp
from jax import lax
from jax.experimental import pallas as pl
from jax.experimental.pallas import tpu as pltpu
from jax.sharding import PartitionSpec as P

MESH = pl.DeviceIdType.MESH
LANES = 128


def kernel(
    count, group, subgroups, width, blocks,
    probes_hbm, gate_hbm, up_hbm, owner_hbm, seeds_hbm,
    digest_ref, hidden_ref,
    owner_ref, seeds_ref, x, gate, up, stage, got, part, part_in, total, plane_out, plane_in, dig_out, dig_in,
    x_load, load_sem, x_send, x_recv, p_send, p_recv, z_send, z_recv, d_send, d_recv,
):
    planes = count // group
    rows = x.shape[1]
    local_rows = gate.shape[0]
    nb = local_rows // LANES
    ranks = dig_out.shape[0]
    dig_rows = dig_out.shape[1]
    me = lax.axis_index("fsdp")
    plane, spot = me // group, me % group

    def peer(index):
        return {"fsdp": index}

    def remote(src, dst, send, recv, index):
        return pltpu.make_async_remote_copy(
            src_ref=src, dst_ref=dst, send_sem=send, recv_sem=recv,
            device_id=peer(index), device_id_type=MESH,
        )

    load_owner = pltpu.make_async_copy(owner_hbm, owner_ref, load_sem.at[2])
    load_seeds = pltpu.make_async_copy(seeds_hbm, seeds_ref, load_sem.at[3])
    load_owner.start()

    def load_x(block):
        columns = pl.ds(pl.multiple_of(block * LANES, LANES), LANES)
        return pltpu.make_async_copy(probes_hbm.at[:, columns], x.at[block], x_load.at[block])

    def start_x(block, carry):
        load_x(block).start()
        return carry

    def wait_x(block, carry):
        load_x(block).wait()
        return carry

    lax.fori_loop(0, blocks, start_x, 0)
    load_gate = pltpu.make_async_copy(gate_hbm, gate, load_sem.at[0])
    load_up = pltpu.make_async_copy(up_hbm, up, load_sem.at[1])
    load_gate.start()
    load_up.start()
    load_seeds.start()

    barrier = pltpu.get_barrier_semaphore()

    def greet(step, carry):
        pl.semaphore_signal(
            barrier, inc=1, device_id=peer((me + step) % count), device_id_type=MESH
        )
        return carry

    lax.fori_loop(1, count, greet, 0)
    load_owner.wait()
    lax.fori_loop(0, blocks, wait_x, 0)

    def pick(target, into):
        for i in range(nb):
            block = owner_ref[target * nb + i]
            into[target, :, i * LANES : (i + 1) * LANES] = x[block]


    def x_copy(target):
        return remote(stage.at[target], got.at[me], x_send.at[target], x_recv.at[me], target)

    def x_arrival(source):
        return remote(stage.at[source], got.at[source], x_send.at[source], x_recv.at[source], source)

    pl.semaphore_wait(barrier, count - 1)
    def partner(m):
        other = plane * 0
        for bit in range((planes - 1).bit_length()):
            digit = (plane // 2**bit) % 2
            other = other + 2**bit * (1 - digit if (m >> bit) & 1 else digit)
        return other

    def send(m, j):
        target = partner(m) * group + (spot + j) % group
        pick(target, stage)
        x_copy(target).start()

    def send_phase(m, last):
        def one(j, carry):
            send(m, j)
            return carry

        lax.fori_loop(1, last, one, 0)

    send_phase(2, group + 1)
    send_phase(0, group)
    send_phase(1, group + 1)
    pick(me, got)

    def squares(block, acc):
        wide = x[block].astype(jnp.float32)
        return acc + wide * wide

    acc = lax.fori_loop(0, blocks, squares, jnp.zeros((rows, LANES), jnp.float32))
    meansq = jnp.sum(acc, axis=1, keepdims=True) / (blocks * LANES)
    scale = 1.0 / jnp.sqrt(meansq + 1e-05)

    load_seeds.wait()
    row_id = lax.broadcasted_iota(jnp.int32, (16, LANES), 0)
    for_gate, for_up = [], []
    for i in range(nb):
        held = lax.broadcasted_iota(jnp.int32, seeds_ref.shape, 0) == owner_ref[me * nb + i]
        seeds = jnp.sum(jnp.where(held, seeds_ref[...], 0), axis=0, keepdims=True)
        signs = jnp.broadcast_to(8 * (1 - 2 * seeds), (16, LANES)).astype(jnp.float32)
        for_gate.append(jnp.where(row_id == i, signs, 0.0))
        for_up.append(jnp.where(row_id == nb + i, signs, 0.0))
    for_gate = jnp.concatenate(for_gate, axis=1).astype(jnp.bfloat16)
    for_up = jnp.concatenate(for_up, axis=1).astype(jnp.bfloat16)
    load_gate.wait()
    load_up.wait()

    def columns_of(t):
        return pl.ds(pl.multiple_of(t * width, width), width)

    def sketch(t, carry):
        both = jnp.dot(for_gate, gate[:, columns_of(t)], preferred_element_type=jnp.float32)
        both += jnp.dot(for_up, up[:, columns_of(t)], preferred_element_type=jnp.float32)
        dig_out[t] = both[:dig_rows]
        return carry

    lax.fori_loop(0, ranks, sketch, 0)
    dig_in[me] = dig_out[me // subgroups]

    def d_copy(target):
        return remote(
            dig_out.at[target // subgroups], dig_in.at[me], d_send.at[target], d_recv.at[me], target
        )

    def d_arrival(source):
        return remote(
            dig_out.at[source // subgroups], dig_in.at[source], d_send.at[source],
            d_recv.at[source], source,
        )

    def send_digest(step, carry):
        d_copy((me + step) % count).start()
        return carry

    lax.fori_loop(1, count, send_digest, 0)

    def product(source):
        rows_of = got[source]
        columns = columns_of(source // subgroups)
        return (
            jnp.dot(rows_of, gate[:, columns], preferred_element_type=jnp.float32),
            jnp.dot(rows_of, up[:, columns], preferred_element_type=jnp.float32),
        )

    def p_copy(source_plane, spot_to):
        return remote(
            part.at[source_plane * group + spot_to],
            part_in.at[source_plane * group + spot],
            p_send.at[source_plane * group + spot_to],
            p_recv.at[source_plane * group + spot],
            plane * group + spot_to,
        )

    def p_arrival(source_plane, spot_from):
        index = source_plane * group + spot_from
        return remote(
            part.at[index], part_in.at[index], p_send.at[index], p_recv.at[index],
            plane * group + spot_from,
        )

    def z_copy(m):
        return remote(
            plane_out.at[m], plane_in.at[m], z_send.at[m], z_recv.at[m],
            partner(m if m % 2 else 1) * group + spot,
        )

    def multiply_other(m, spot_from):
        source = partner(m) * group + spot_from
        a, b = product(source)
        part[source, :, :width] = a.astype(jnp.bfloat16)
        part[source, :, width:] = b.astype(jnp.bfloat16)
        p_copy(partner(m), spot_from).start()

    def multiply_own(m):
        a, b = product(partner(m) * group + spot)
        total[m, :, :width] = a
        total[m, :, width:] = b

    def start_following(m, j):
        if m >= 2 and m + 1 < planes:
            if m % 2:
                send(m + 1, j)
            else:
                @pl.when((j - 1) // 2 == spot % 2)
                def _():
                    send(m + 1, 2 * ((j - 1) % 2) + 1)
                    send(m + 1, 2 * ((j - 1) % 2) + 2)

    def multiply(m):
        def others(j, carry):
            spot_from = (spot + group - j) % group
            x_arrival(partner(m) * group + spot_from).wait_recv()
            start_following(m, j)
            multiply_other(m, spot_from)
            return carry

        lax.fori_loop(1, group, others, 0)
        if m != 0:
            x_arrival(partner(m) * group + spot).wait_recv()
            start_following(m, group)
        multiply_own(m)

    def multiply_staggered(m):
        for half in range(2):
            def one(step, carry, half=half):
                j = 2 - (spot + half) % 2 + 2 * step
                spot_from = (spot + group - j) % group
                x_arrival(partner(m) * group + spot_from).wait_recv()
                start_following(m, 2 * half + step + 1)

                @pl.when(j == group)
                def _():
                    multiply_own(m)

                @pl.when(j != group)
                def _():
                    multiply_other(m, spot_from)

                return carry

            lax.fori_loop(0, 2, one, 0)

            @pl.when(spot % 2 == half)
            def _():
                reduce(m)

    def reduce(m):
        summed = total[m]
        for j in range(1, group):
            spot_from = (spot + group - j) % group
            p_arrival(partner(m), spot_from).wait_recv()
        if m > 2 and m % 2:
            z_copy(m - 1).wait_recv()
            summed += plane_in[m - 1].astype(jnp.float32)
        for j in range(1, group):
            spot_from = (spot + group - j) % group
            summed += part_in[partner(m) * group + spot_from].astype(jnp.float32)
        if m > 0:
            plane_out[m] = summed.astype(jnp.bfloat16)
            z_copy(m).start()
        else:
            total[m] = summed

    multiply(0)
    multiply(2)
    reduce(0)
    multiply(1)
    reduce(2)
    reduce(1)
    for m in range(3, planes):
        if m % 2:
            multiply_staggered(m)
        else:
            multiply(m)
            reduce(m)

    def wait_digest(step, carry):
        d_arrival((me + step) % count).wait_recv()
        return carry

    lax.fori_loop(1, count, wait_digest, 0)
    span = count * dig_rows
    column = lax.broadcasted_iota(jnp.int32, (8, span), 1)
    inner = column % dig_rows
    place = jnp.where(inner < 2 * nb, (column // dig_rows) * nb + inner % nb, -1)
    owners = jnp.full((8, span), -1, jnp.int32)
    for j in range(blocks):
        owners = jnp.where(place == j, owner_ref[j], owners)
    owners = owners + jnp.where(inner >= nb, blocks, 0)
    owners = jnp.where(inner < 2 * nb, owners, -1)
    wanted = lax.broadcasted_iota(jnp.int32, (2 * blocks, span), 0)
    chosen = jnp.where(jnp.broadcast_to(owners[:1], (2 * blocks, span)) == wanted, 1.0, 0.0)
    digest_ref[...] = jnp.dot(
        chosen, dig_in[...].reshape(span, width),
        precision=lax.Precision.HIGHEST, preferred_element_type=jnp.float32,
    )

    summed = total[0]
    for m in range(1, planes, 2):
        z_copy(m).wait_recv()
        summed += plane_in[m].astype(jnp.float32)
    gate_sum = summed[:, :width] * scale
    up_sum = summed[:, width:] * scale
    hidden_ref[...] = (gate_sum / (1.0 + jnp.exp(-gate_sum)) * up_sum).astype(jnp.bfloat16)

    def drain(step, carry):
        target = (me + step) % count
        x_copy(target).wait_send()
        d_copy(target).wait_send()
        return carry

    lax.fori_loop(1, count, drain, 0)

    def drain_plane(source_plane, carry):
        def drain_spot(j, inner_carry):
            p_copy(source_plane, (spot + group - j) % group).wait_send()
            return inner_carry

        return lax.fori_loop(1, group, drain_spot, carry)

    lax.fori_loop(0, planes, drain_plane, 0)

    for m in range(1, planes):
        z_copy(m).wait_send()


def on_device(trainer_gate, trainer_up, owner_map, sketch_seeds, probes):
    local_rows, _, slice_width = trainer_gate.shape
    count = lax.axis_size("fsdp")
    ranks = min(16, count)
    subgroups = count // ranks
    width = slice_width // ranks
    narrow = width // subgroups
    group = 4
    planes = count // group
    total_rows = local_rows * count
    blocks = total_rows // LANES
    nb = local_rows // LANES
    dig_rows = -(-2 * nb // 8) * 8
    rows = probes.shape[2]
    bf16, f32 = jnp.bfloat16, jnp.float32
    dma = pltpu.SemaphoreType.DMA
    digest, hidden = pl.pallas_call(
        functools.partial(kernel, count, group, subgroups, width, blocks),
        out_shape=(
            jax.ShapeDtypeStruct((2 * blocks, width), f32),
            jax.ShapeDtypeStruct((rows, width), bf16),
        ),
        in_specs=[pl.BlockSpec(memory_space=pl.ANY)] * 5,
        out_specs=[pl.BlockSpec(memory_space=pltpu.VMEM)] * 2,
        scratch_shapes=[
            pltpu.SMEM((blocks,), jnp.int32),
            pltpu.VMEM((blocks, LANES), jnp.int32),
            pltpu.VMEM((blocks, rows, LANES), bf16),
            pltpu.VMEM((local_rows, slice_width), bf16),
            pltpu.VMEM((local_rows, slice_width), bf16),
            pltpu.VMEM((count, rows, local_rows), bf16),
            pltpu.VMEM((count, rows, local_rows), bf16),
            pltpu.VMEM((count, rows, 2 * width), bf16),
            pltpu.VMEM((count, rows, 2 * width), bf16),
            pltpu.VMEM((planes, rows, 2 * width), f32),
            pltpu.VMEM((planes, rows, 2 * width), bf16),
            pltpu.VMEM((planes, rows, 2 * width), bf16),
            pltpu.VMEM((ranks, dig_rows, width), f32),
            pltpu.VMEM((count, dig_rows, width), f32),
            dma((blocks,)), dma((4,)),
            dma((count,)), dma((count,)),
            dma((count,)), dma((count,)),
            dma((planes,)), dma((planes,)),
            dma((count,)), dma((count,)),
        ],
        compiler_params=pltpu.CompilerParams(
            collective_id=0, has_side_effects=True, vmem_limit_bytes=60 * 2**20
        ),
    )(
        probes.reshape(rows, total_rows),
        trainer_gate.reshape(local_rows, slice_width),
        trainer_up.reshape(local_rows, slice_width),
        owner_map,
        sketch_seeds.reshape(blocks, LANES),
    )
    if subgroups > 1:
        member = lax.axis_index("fsdp")
        digest = lax.dynamic_slice_in_dim(digest, (member % subgroups) * narrow, narrow, 1)
    return (
        digest.reshape(2, blocks, 1, narrow),
        hidden.reshape(1, 1, rows, 1, width),
    )


def solution(mesh):
    placed = (P("fsdp", "dp", None), P("fsdp", "dp", None), P(), P(), P("rep", "fsdp", None, None))
    return jax.shard_map(
        on_device,
        mesh=mesh,
        in_specs=placed,
        out_specs=(P(None, None, "dp", "fsdp"), P("rep", "fsdp", None, "dp", None)),
        check_vma=False,
    )
```

```python
import functools

import jax
import jax.numpy as jnp
from jax import lax
from jax.experimental import pallas as pl
from jax.experimental.pallas import tpu as pltpu
from jax.sharding import PartitionSpec as P

MESH = pl.DeviceIdType.MESH
LANES = 128


def kernel(
    count, group, subgroups, width, blocks,
    probes_hbm, gate_hbm, up_hbm, owner_hbm, seeds_hbm,
    digest_ref, hidden_ref,
    owner_ref, seeds_ref, x, gate, up, stage, got, part, part_in, total, plane_out, plane_in, dig_out, dig_in,
    x_load, load_sem, x_send, x_recv, p_send, p_recv, z_send, z_recv, d_send, d_recv,
):
    planes = count // group
    rows = x.shape[1]
    local_rows = gate.shape[0]
    nb = local_rows // LANES
    ranks = dig_out.shape[0]
    dig_rows = dig_out.shape[1]
    me = lax.axis_index("fsdp")
    plane, spot = me // group, me % group

    def peer(index):
        return {"fsdp": index}

    def remote(src, dst, send, recv, index):
        return pltpu.make_async_remote_copy(
            src_ref=src, dst_ref=dst, send_sem=send, recv_sem=recv,
            device_id=peer(index), device_id_type=MESH,
        )

    load_owner = pltpu.make_async_copy(owner_hbm, owner_ref, load_sem.at[2])
    load_seeds = pltpu.make_async_copy(seeds_hbm, seeds_ref, load_sem.at[3])
    load_owner.start()

    def load_x(block):
        columns = pl.ds(pl.multiple_of(block * LANES, LANES), LANES)
        return pltpu.make_async_copy(probes_hbm.at[:, columns], x.at[block], x_load.at[block])

    def start_x(block, carry):
        load_x(block).start()
        return carry

    def wait_x(block, carry):
        load_x(block).wait()
        return carry

    lax.fori_loop(0, blocks, start_x, 0)
    load_gate = pltpu.make_async_copy(gate_hbm, gate, load_sem.at[0])
    load_up = pltpu.make_async_copy(up_hbm, up, load_sem.at[1])
    load_gate.start()
    load_up.start()
    load_seeds.start()

    barrier = pltpu.get_barrier_semaphore()

    def greet(step, carry):
        pl.semaphore_signal(
            barrier, inc=1, device_id=peer((me + step) % count), device_id_type=MESH
        )
        return carry

    lax.fori_loop(1, count, greet, 0)
    load_owner.wait()
    lax.fori_loop(0, blocks, wait_x, 0)

    def pick(target, into):
        for i in range(nb):
            block = owner_ref[target * nb + i]
            into[target, :, i * LANES : (i + 1) * LANES] = x[block]


    def x_copy(target):
        return remote(stage.at[target], got.at[me], x_send.at[target], x_recv.at[me], target)

    def x_arrival(source):
        return remote(stage.at[source], got.at[source], x_send.at[source], x_recv.at[source], source)

    pl.semaphore_wait(barrier, count - 1)
    def partner(m):
        other = plane * 0
        for bit in range((planes - 1).bit_length()):
            digit = (plane // 2**bit) % 2
            other = other + 2**bit * (1 - digit if (m >> bit) & 1 else digit)
        return other

    def send(m, j):
        target = partner(m) * group + (spot + j) % group
        pick(target, stage)
        x_copy(target).start()

    def send_phase(m, last):
        def one(j, carry):
            send(m, j)
            return carry

        lax.fori_loop(1, last, one, 0)

    send_phase(2, group + 1)
    send_phase(0, group)
    send_phase(1, group + 1)

    @pl.when(spot % 2 == 0)
    def _():
        send_phase(3, group + 1)

    pick(me, got)

    def squares(block, acc):
        wide = x[block].astype(jnp.float32)
        return acc + wide * wide

    acc = lax.fori_loop(0, blocks, squares, jnp.zeros((rows, LANES), jnp.float32))
    meansq = jnp.sum(acc, axis=1, keepdims=True) / (blocks * LANES)
    scale = 1.0 / jnp.sqrt(meansq + 1e-05)

    load_seeds.wait()
    row_id = lax.broadcasted_iota(jnp.int32, (16, LANES), 0)
    for_gate, for_up = [], []
    for i in range(nb):
        held = lax.broadcasted_iota(jnp.int32, seeds_ref.shape, 0) == owner_ref[me * nb + i]
        seeds = jnp.sum(jnp.where(held, seeds_ref[...], 0), axis=0, keepdims=True)
        signs = jnp.broadcast_to(8 * (1 - 2 * seeds), (16, LANES)).astype(jnp.float32)
        for_gate.append(jnp.where(row_id == i, signs, 0.0))
        for_up.append(jnp.where(row_id == nb + i, signs, 0.0))
    for_gate = jnp.concatenate(for_gate, axis=1).astype(jnp.bfloat16)
    for_up = jnp.concatenate(for_up, axis=1).astype(jnp.bfloat16)
    load_gate.wait()
    load_up.wait()

    def columns_of(t):
        return pl.ds(pl.multiple_of(t * width, width), width)

    def sketch(t, carry):
        both = jnp.dot(for_gate, gate[:, columns_of(t)], preferred_element_type=jnp.float32)
        both += jnp.dot(for_up, up[:, columns_of(t)], preferred_element_type=jnp.float32)
        dig_out[t] = both[:dig_rows]
        return carry

    lax.fori_loop(0, ranks, sketch, 0)
    dig_in[me] = dig_out[me // subgroups]

    def d_copy(target):
        return remote(
            dig_out.at[target // subgroups], dig_in.at[me], d_send.at[target], d_recv.at[me], target
        )

    def d_arrival(source):
        return remote(
            dig_out.at[source // subgroups], dig_in.at[source], d_send.at[source],
            d_recv.at[source], source,
        )

    def send_digest(step, carry):
        d_copy((me + step) % count).start()
        return carry

    lax.fori_loop(1, count, send_digest, 0)

    def product(source):
        rows_of = got[source]
        columns = columns_of(source // subgroups)
        return (
            jnp.dot(rows_of, gate[:, columns], preferred_element_type=jnp.float32),
            jnp.dot(rows_of, up[:, columns], preferred_element_type=jnp.float32),
        )

    def p_copy(source_plane, spot_to):
        return remote(
            part.at[source_plane * group + spot_to],
            part_in.at[source_plane * group + spot],
            p_send.at[source_plane * group + spot_to],
            p_recv.at[source_plane * group + spot],
            plane * group + spot_to,
        )

    def p_arrival(source_plane, spot_from):
        index = source_plane * group + spot_from
        return remote(
            part.at[index], part_in.at[index], p_send.at[index], p_recv.at[index],
            plane * group + spot_from,
        )

    def z_copy(m):
        return remote(
            plane_out.at[m], plane_in.at[m], z_send.at[m], z_recv.at[m],
            partner(m if m % 2 else 1) * group + spot,
        )

    def multiply_other(m, spot_from):
        source = partner(m) * group + spot_from
        a, b = product(source)
        part[source, :, :width] = a.astype(jnp.bfloat16)
        part[source, :, width:] = b.astype(jnp.bfloat16)
        p_copy(partner(m), spot_from).start()

    def multiply_own(m):
        a, b = product(partner(m) * group + spot)
        total[m, :, :width] = a
        total[m, :, width:] = b

    def start_following(m, j):
        if m >= 2 and m + 1 < planes:
            if m % 2:
                send(m + 1, j)
            else:
                turn = (1 - spot % 2) * 2 if m == 2 else spot % 2

                @pl.when((j - 1) // 2 == turn)
                def _():
                    send(m + 1, 2 * ((j - 1) % 2) + 1)
                    send(m + 1, 2 * ((j - 1) % 2) + 2)

    def multiply(m):
        def others(j, carry):
            spot_from = (spot + group - j) % group
            x_arrival(partner(m) * group + spot_from).wait_recv()
            start_following(m, j)
            multiply_other(m, spot_from)
            return carry

        lax.fori_loop(1, group, others, 0)
        if m != 0:
            x_arrival(partner(m) * group + spot).wait_recv()
            start_following(m, group)
        multiply_own(m)

    def multiply_staggered(m):
        for half in range(2):
            def one(step, carry, half=half):
                j = 2 - (spot + half) % 2 + 2 * step
                spot_from = (spot + group - j) % group
                x_arrival(partner(m) * group + spot_from).wait_recv()
                start_following(m, 2 * half + step + 1)

                @pl.when(j == group)
                def _():
                    multiply_own(m)

                @pl.when(j != group)
                def _():
                    multiply_other(m, spot_from)

                return carry

            lax.fori_loop(0, 2, one, 0)

            @pl.when(spot % 2 == half)
            def _():
                reduce(m)

    def reduce(m):
        summed = total[m]
        for j in range(1, group):
            spot_from = (spot + group - j) % group
            p_arrival(partner(m), spot_from).wait_recv()
        if m > 2 and m % 2:
            z_copy(m - 1).wait_recv()
            summed += plane_in[m - 1].astype(jnp.float32)
        for j in range(1, group):
            spot_from = (spot + group - j) % group
            summed += part_in[partner(m) * group + spot_from].astype(jnp.float32)
        if m > 0:
            plane_out[m] = summed.astype(jnp.bfloat16)
            z_copy(m).start()
        else:
            total[m] = summed

    multiply(0)
    multiply(2)
    reduce(0)
    multiply(1)
    reduce(2)
    reduce(1)
    for m in range(3, planes):
        if m % 2:
            multiply_staggered(m)
        else:
            multiply(m)
            reduce(m)

    def wait_digest(step, carry):
        d_arrival((me + step) % count).wait_recv()
        return carry

    lax.fori_loop(1, count, wait_digest, 0)
    span = count * dig_rows
    column = lax.broadcasted_iota(jnp.int32, (8, span), 1)
    inner = column % dig_rows
    place = jnp.where(inner < 2 * nb, (column // dig_rows) * nb + inner % nb, -1)
    owners = jnp.full((8, span), -1, jnp.int32)
    for j in range(blocks):
        owners = jnp.where(place == j, owner_ref[j], owners)
    owners = owners + jnp.where(inner >= nb, blocks, 0)
    owners = jnp.where(inner < 2 * nb, owners, -1)
    wanted = lax.broadcasted_iota(jnp.int32, (2 * blocks, span), 0)
    chosen = jnp.where(jnp.broadcast_to(owners[:1], (2 * blocks, span)) == wanted, 1.0, 0.0)
    digest_ref[...] = jnp.dot(
        chosen, dig_in[...].reshape(span, width),
        precision=lax.Precision.HIGHEST, preferred_element_type=jnp.float32,
    )

    summed = total[0]
    for m in range(1, planes, 2):
        z_copy(m).wait_recv()
        summed += plane_in[m].astype(jnp.float32)
    gate_sum = summed[:, :width] * scale
    up_sum = summed[:, width:] * scale
    hidden_ref[...] = (gate_sum / (1.0 + jnp.exp(-gate_sum)) * up_sum).astype(jnp.bfloat16)

    def drain(step, carry):
        target = (me + step) % count
        x_copy(target).wait_send()
        d_copy(target).wait_send()
        return carry

    lax.fori_loop(1, count, drain, 0)

    def drain_plane(source_plane, carry):
        def drain_spot(j, inner_carry):
            p_copy(source_plane, (spot + group - j) % group).wait_send()
            return inner_carry

        return lax.fori_loop(1, group, drain_spot, carry)

    lax.fori_loop(0, planes, drain_plane, 0)

    for m in range(1, planes):
        z_copy(m).wait_send()


def on_device(trainer_gate, trainer_up, owner_map, sketch_seeds, probes):
    local_rows, _, slice_width = trainer_gate.shape
    count = lax.axis_size("fsdp")
    ranks = min(16, count)
    subgroups = count // ranks
    width = slice_width // ranks
    narrow = width // subgroups
    group = 4
    planes = count // group
    total_rows = local_rows * count
    blocks = total_rows // LANES
    nb = local_rows // LANES
    dig_rows = -(-2 * nb // 8) * 8
    rows = probes.shape[2]
    bf16, f32 = jnp.bfloat16, jnp.float32
    dma = pltpu.SemaphoreType.DMA
    digest, hidden = pl.pallas_call(
        functools.partial(kernel, count, group, subgroups, width, blocks),
        out_shape=(
            pltpu.VMEM((2 * blocks, width), f32),
            pltpu.VMEM((rows, width), bf16),
        ),
        in_specs=[pl.BlockSpec(memory_space=pl.ANY)] * 5,
        out_specs=[pl.BlockSpec(memory_space=pltpu.VMEM)] * 2,
        scratch_shapes=[
            pltpu.SMEM((blocks,), jnp.int32),
            pltpu.VMEM((blocks, LANES), jnp.int32),
            pltpu.VMEM((blocks, rows, LANES), bf16),
            pltpu.VMEM((local_rows, slice_width), bf16),
            pltpu.VMEM((local_rows, slice_width), bf16),
            pltpu.VMEM((count, rows, local_rows), bf16),
            pltpu.VMEM((count, rows, local_rows), bf16),
            pltpu.VMEM((count, rows, 2 * width), bf16),
            pltpu.VMEM((count, rows, 2 * width), bf16),
            pltpu.VMEM((planes, rows, 2 * width), f32),
            pltpu.VMEM((planes, rows, 2 * width), bf16),
            pltpu.VMEM((planes, rows, 2 * width), bf16),
            pltpu.VMEM((ranks, dig_rows, width), f32),
            pltpu.VMEM((count, dig_rows, width), f32),
            dma((blocks,)), dma((4,)),
            dma((count,)), dma((count,)),
            dma((count,)), dma((count,)),
            dma((planes,)), dma((planes,)),
            dma((count,)), dma((count,)),
        ],
        compiler_params=pltpu.CompilerParams(
            collective_id=0, has_side_effects=True, vmem_limit_bytes=60 * 2**20
        ),
    )(
        probes.reshape(rows, total_rows),
        trainer_gate.reshape(local_rows, slice_width),
        trainer_up.reshape(local_rows, slice_width),
        owner_map,
        sketch_seeds.reshape(blocks, LANES),
    )
    if subgroups > 1:
        member = lax.axis_index("fsdp")
        digest = lax.dynamic_slice_in_dim(digest, (member % subgroups) * narrow, narrow, 1)
    return (
        digest.reshape(2, blocks, 1, narrow),
        hidden.reshape(1, 1, rows, 1, width),
    )


def solution(mesh):
    placed = (P("fsdp", "dp", None), P("fsdp", "dp", None), P(), P(), P("rep", "fsdp", None, None))
    return jax.shard_map(
        on_device,
        mesh=mesh,
        in_specs=placed,
        out_specs=(P(None, None, "dp", "fsdp"), P("rep", "fsdp", None, "dp", None)),
        check_vma=False,
    )
```

```python
import functools

import jax
import jax.numpy as jnp
from jax import lax
from jax.experimental import pallas as pl
from jax.experimental.pallas import tpu as pltpu
from jax.sharding import PartitionSpec as P

MESH = pl.DeviceIdType.MESH
LANES = 128


def kernel(
    count, group, subgroups, width, blocks,
    probes_hbm, gate_hbm, up_hbm, owner_hbm, seeds_hbm,
    digest_ref, hidden_ref,
    owner_ref, seeds_ref, x_flat, x, gate, up, stage, got, part, part_in, total, plane_out, plane_in, dig_out, dig_in,
    x_load, load_sem, x_send, x_recv, p_send, p_recv, z_send, z_recv, d_send, d_recv,
):
    planes = count // group
    rows = x.shape[1]
    local_rows = gate.shape[0]
    nb = local_rows // LANES
    ranks = dig_out.shape[0]
    dig_rows = dig_out.shape[1]
    me = lax.axis_index("fsdp")
    plane, spot = me // group, me % group

    def peer(index):
        return {"fsdp": index}

    def remote(src, dst, send, recv, index):
        return pltpu.make_async_remote_copy(
            src_ref=src, dst_ref=dst, send_sem=send, recv_sem=recv,
            device_id=peer(index), device_id_type=MESH,
        )

    barrier = pltpu.get_barrier_semaphore()

    def greet(step, carry):
        pl.semaphore_signal(
            barrier, inc=1, device_id=peer((me + step) % count), device_id_type=MESH
        )
        return carry

    load_owner = pltpu.make_async_copy(owner_hbm, owner_ref, load_sem.at[2])
    load_seeds = pltpu.make_async_copy(seeds_hbm, seeds_ref, load_sem.at[3])
    load_gate = pltpu.make_async_copy(gate_hbm, gate, load_sem.at[0])
    load_up = pltpu.make_async_copy(up_hbm, up, load_sem.at[1])
    quarter = blocks // 4
    loads = []
    for c in range(4):
        columns = pl.ds(c * quarter * LANES, quarter * LANES)
        loads.append(
            pltpu.make_async_copy(probes_hbm.at[:, columns], x_flat.at[:, columns], x_load.at[c])
        )
    load_owner.start()
    for load in loads:
        load.start()
    lax.fori_loop(1, count, greet, 0)
    load_gate.start()
    load_up.start()
    load_seeds.start()
    for c in range(4):
        loads[c].wait()
        for block in range(c * quarter, (c + 1) * quarter):
            x[block] = x_flat[:, block * LANES : (block + 1) * LANES]
    load_owner.wait()

    def pick(target, into):
        for i in range(nb):
            block = owner_ref[target * nb + i]
            into[target, :, i * LANES : (i + 1) * LANES] = x[block]


    half_rows = rows // 2

    def rows_of(half):
        return pl.ds(0, rows) if half is None else pl.ds(half * half_rows, half_rows)

    def slot(index, half):
        return index + count if half == 1 else index

    def halves(m):
        return (0, 1) if m > 2 and m % 2 else (None,)

    def x_copy(target, half=None):
        return remote(
            stage.at[target, rows_of(half)], got.at[me, rows_of(half)],
            x_send.at[slot(target, half)], x_recv.at[slot(me, half)], target,
        )

    def x_arrival(source, half=None):
        return remote(
            stage.at[source, rows_of(half)], got.at[source, rows_of(half)],
            x_send.at[slot(source, half)], x_recv.at[slot(source, half)], source,
        )

    pl.semaphore_wait(barrier, count - 1)
    def partner(m):
        other = plane * 0
        for bit in range((planes - 1).bit_length()):
            digit = (plane // 2**bit) % 2
            other = other + 2**bit * (1 - digit if (m >> bit) & 1 else digit)
        return other

    def target_of(m, j):
        return partner(m) * group + (spot + j) % group

    def send(m, j, half=None):
        if half != 1:
            pick(target_of(m, j), stage)
        x_copy(target_of(m, j), half).start()

    def send_phase(m, last, half=None):
        def one(j, carry):
            send(m, j, half)
            return carry

        lax.fori_loop(1, last, one, 0)

    send_phase(2, group + 1)
    send_phase(0, group)
    send_phase(1, group + 1)

    @pl.when(spot % 2 == 0)
    def _():
        send_phase(3, group + 1, 0)
        send_phase(3, group + 1, 1)

    pick(me, got)

    def squares(block, acc):
        wide = x[block].astype(jnp.float32)
        return acc + wide * wide

    acc = lax.fori_loop(0, blocks, squares, jnp.zeros((rows, LANES), jnp.float32))
    meansq = jnp.sum(acc, axis=1, keepdims=True) / (blocks * LANES)
    scale = 1.0 / jnp.sqrt(meansq + 1e-05)

    load_seeds.wait()
    row_id = lax.broadcasted_iota(jnp.int32, (16, LANES), 0)
    for_gate, for_up = [], []
    for i in range(nb):
        held = lax.broadcasted_iota(jnp.int32, seeds_ref.shape, 0) == owner_ref[me * nb + i]
        seeds = jnp.sum(jnp.where(held, seeds_ref[...], 0), axis=0, keepdims=True)
        signs = jnp.broadcast_to(8 * (1 - 2 * seeds), (16, LANES)).astype(jnp.float32)
        for_gate.append(jnp.where(row_id == i, signs, 0.0))
        for_up.append(jnp.where(row_id == nb + i, signs, 0.0))
    for_gate = jnp.concatenate(for_gate, axis=1).astype(jnp.bfloat16)
    for_up = jnp.concatenate(for_up, axis=1).astype(jnp.bfloat16)
    load_gate.wait()
    load_up.wait()

    def columns_of(t):
        return pl.ds(pl.multiple_of(t * width, width), width)

    def sketch(t, carry):
        both = jnp.dot(for_gate, gate[:, columns_of(t)], preferred_element_type=jnp.float32)
        both += jnp.dot(for_up, up[:, columns_of(t)], preferred_element_type=jnp.float32)
        dig_out[t] = both[:dig_rows]
        return carry

    lax.fori_loop(0, ranks, sketch, 0)
    dig_in[me] = dig_out[me // subgroups]

    def d_copy(target):
        return remote(
            dig_out.at[target // subgroups], dig_in.at[me], d_send.at[target], d_recv.at[me], target
        )

    def d_arrival(source):
        return remote(
            dig_out.at[source // subgroups], dig_in.at[source], d_send.at[source],
            d_recv.at[source], source,
        )

    def send_digest(step, carry):
        d_copy((me + step) % count).start()
        return carry

    lax.fori_loop(1, count, send_digest, 0)

    def product(source, half=None):
        rows_in = got[source, rows_of(half)]
        columns = columns_of(source // subgroups)
        return (
            jnp.dot(rows_in, gate[:, columns], preferred_element_type=jnp.float32),
            jnp.dot(rows_in, up[:, columns], preferred_element_type=jnp.float32),
        )

    def p_copy(source_plane, spot_to, half=None):
        index, here = source_plane * group + spot_to, source_plane * group + spot
        return remote(
            part.at[index, rows_of(half)], part_in.at[here, rows_of(half)],
            p_send.at[slot(index, half)], p_recv.at[slot(here, half)],
            plane * group + spot_to,
        )

    def p_arrival(source_plane, spot_from, half=None):
        index = source_plane * group + spot_from
        return remote(
            part.at[index, rows_of(half)], part_in.at[index, rows_of(half)],
            p_send.at[slot(index, half)], p_recv.at[slot(index, half)],
            plane * group + spot_from,
        )

    def z_copy(m, half=None):
        index = m + planes if half == 1 else m
        return remote(
            plane_out.at[m, rows_of(half)], plane_in.at[m, rows_of(half)],
            z_send.at[index], z_recv.at[index],
            partner(m if m % 2 else 1) * group + spot,
        )

    def multiply_other(m, spot_from, half=None):
        source = partner(m) * group + spot_from
        a, b = product(source, half)
        part[source, rows_of(half), :width] = a.astype(jnp.bfloat16)
        part[source, rows_of(half), width:] = b.astype(jnp.bfloat16)
        p_copy(partner(m), spot_from, half).start()

    def multiply_own(m, half=None):
        a, b = product(partner(m) * group + spot, half)
        total[m, rows_of(half), :width] = a
        total[m, rows_of(half), width:] = b

    def start_following(m, j):
        if m >= 2 and m + 1 < planes:
            if m % 2:
                send(m + 1, j)
                return
            for half in halves(m + 1):
                if m == 2:
                    turn = (spot % 2) * (half + 1)
                else:
                    turn = 2 * (spot % 2) + half + 1

                @pl.when(j == turn)
                def _():
                    send_phase(m + 1, group + 1, half)

    def multiply(m):
        def others(j, carry):
            spot_from = (spot + group - j) % group
            x_arrival(partner(m) * group + spot_from).wait_recv()
            start_following(m, j)
            multiply_other(m, spot_from)
            return carry

        lax.fori_loop(1, group, others, 0)
        if m != 0:
            x_arrival(partner(m) * group + spot).wait_recv()
            start_following(m, group)
        multiply_own(m)

    def multiply_staggered(m):
        for odd in range(2):
            for half in halves(m):
                def one(step, carry, odd=odd, half=half):
                    j = 2 - (spot + odd) % 2 + 2 * step
                    spot_from = (spot + group - j) % group
                    x_arrival(partner(m) * group + spot_from, half).wait_recv()
                    if half == 1:
                        start_following(m, 2 * odd + step + 1)

                    @pl.when(j == group)
                    def _():
                        multiply_own(m, half)

                    @pl.when(j != group)
                    def _():
                        multiply_other(m, spot_from, half)

                    return carry

                lax.fori_loop(0, 2, one, 0)

                @pl.when(spot % 2 == odd)
                def _():
                    reduce(m, half)

    def reduce(m, half=None):
        summed = total[m, rows_of(half)]
        if m > 2 and m % 2:
            if half == 0:
                z_copy(m - 1).wait_recv()
            summed += plane_in[m - 1, rows_of(half)].astype(jnp.float32)
        for j in range(1, group):
            p_arrival(partner(m), (spot + group - j) % group, half).wait_recv()
        for j in range(1, group):
            index = partner(m) * group + (spot + group - j) % group
            summed += part_in[index, rows_of(half)].astype(jnp.float32)
        if m > 0:
            plane_out[m, rows_of(half)] = summed.astype(jnp.bfloat16)
            z_copy(m, half).start()
        else:
            total[m] = summed

    multiply(0)
    multiply(2)
    reduce(0)
    multiply(1)
    reduce(2)
    reduce(1)
    for m in range(3, planes):
        if m % 2:
            multiply_staggered(m)
        else:
            multiply(m)
            reduce(m)

    def wait_digest(step, carry):
        d_arrival((me + step) % count).wait_recv()
        return carry

    lax.fori_loop(1, count, wait_digest, 0)
    span = count * dig_rows
    column = lax.broadcasted_iota(jnp.int32, (8, span), 1)
    inner = column % dig_rows
    place = jnp.where(inner < 2 * nb, (column // dig_rows) * nb + inner % nb, -1)
    owners = jnp.full((8, span), -1, jnp.int32)
    for j in range(blocks):
        owners = jnp.where(place == j, owner_ref[j], owners)
    owners = owners + jnp.where(inner >= nb, blocks, 0)
    owners = jnp.where(inner < 2 * nb, owners, -1)
    wanted = lax.broadcasted_iota(jnp.int32, (2 * blocks, span), 0)
    chosen = jnp.where(jnp.broadcast_to(owners[:1], (2 * blocks, span)) == wanted, 1.0, 0.0)
    digest_ref[...] = jnp.dot(
        chosen, dig_in[...].reshape(span, width),
        precision=lax.Precision.HIGHEST, preferred_element_type=jnp.float32,
    )

    def drain_digest(step, carry):
        d_copy((me + step) % count).wait_send()
        return carry

    lax.fori_loop(1, count, drain_digest, 0)
    for m in range(planes):
        for half in halves(m):
            def drain_spot(j, carry, m=m, half=half):
                x_copy(target_of(m, j), half).wait_send()
                return carry

            def drain_part(j, carry, m=m, half=half):
                p_copy(partner(m), (spot + group - j) % group, half).wait_send()
                return carry

            lax.fori_loop(1, group + (m > 0), drain_spot, 0)
            lax.fori_loop(1, group, drain_part, 0)

    z_copy(1).wait_recv()
    for half in range(2):
        summed = total[0, rows_of(half)] + plane_in[1, rows_of(half)].astype(jnp.float32)
        for m in range(3, planes, 2):
            z_copy(m, half).wait_recv()
            summed += plane_in[m, rows_of(half)].astype(jnp.float32)
        factor = scale[half * half_rows : (half + 1) * half_rows]
        gate_sum = summed[:, :width] * factor
        up_sum = summed[:, width:] * factor
        hidden_ref[rows_of(half)] = (
            gate_sum / (1.0 + jnp.exp(-gate_sum)) * up_sum
        ).astype(jnp.bfloat16)

    for m in range(1, planes):
        for half in halves(m):
            z_copy(m, half).wait_send()


def on_device(trainer_gate, trainer_up, owner_map, sketch_seeds, probes):
    local_rows, _, slice_width = trainer_gate.shape
    count = lax.axis_size("fsdp")
    ranks = min(16, count)
    subgroups = count // ranks
    width = slice_width // ranks
    narrow = width // subgroups
    group = 4
    planes = count // group
    total_rows = local_rows * count
    blocks = total_rows // LANES
    nb = local_rows // LANES
    dig_rows = -(-2 * nb // 8) * 8
    rows = probes.shape[2]
    bf16, f32 = jnp.bfloat16, jnp.float32
    dma = pltpu.SemaphoreType.DMA
    digest, hidden = pl.pallas_call(
        functools.partial(kernel, count, group, subgroups, width, blocks),
        out_shape=(
            pltpu.VMEM((2 * blocks, width), f32),
            pltpu.VMEM((rows, width), bf16),
        ),
        in_specs=[pl.BlockSpec(memory_space=pl.ANY)] * 5,
        out_specs=[pl.BlockSpec(memory_space=pltpu.VMEM)] * 2,
        scratch_shapes=[
            pltpu.SMEM((blocks,), jnp.int32),
            pltpu.VMEM((blocks, LANES), jnp.int32),
            pltpu.VMEM((rows, total_rows), bf16),
            pltpu.VMEM((blocks, rows, LANES), bf16),
            pltpu.VMEM((local_rows, slice_width), bf16),
            pltpu.VMEM((local_rows, slice_width), bf16),
            pltpu.VMEM((count, rows, local_rows), bf16),
            pltpu.VMEM((count, rows, local_rows), bf16),
            pltpu.VMEM((count, rows, 2 * width), bf16),
            pltpu.VMEM((count, rows, 2 * width), bf16),
            pltpu.VMEM((planes, rows, 2 * width), f32),
            pltpu.VMEM((planes, rows, 2 * width), bf16),
            pltpu.VMEM((planes, rows, 2 * width), bf16),
            pltpu.VMEM((ranks, dig_rows, width), f32),
            pltpu.VMEM((count, dig_rows, width), f32),
            dma((4,)), dma((4,)),
            dma((2 * count,)), dma((2 * count,)),
            dma((2 * count,)), dma((2 * count,)),
            dma((2 * planes,)), dma((2 * planes,)),
            dma((count,)), dma((count,)),
        ],
        compiler_params=pltpu.CompilerParams(
            collective_id=0, has_side_effects=True, vmem_limit_bytes=60 * 2**20
        ),
    )(
        probes.reshape(rows, total_rows),
        trainer_gate.reshape(local_rows, slice_width),
        trainer_up.reshape(local_rows, slice_width),
        owner_map,
        sketch_seeds.reshape(blocks, LANES),
    )
    if subgroups > 1:
        member = lax.axis_index("fsdp")
        digest = lax.dynamic_slice_in_dim(digest, (member % subgroups) * narrow, narrow, 1)
    return (
        digest.reshape(2, blocks, 1, narrow),
        hidden.reshape(1, 1, rows, 1, width),
    )


def solution(mesh):
    placed = (P("fsdp", "dp", None), P("fsdp", "dp", None), P(), P(), P("rep", "fsdp", None, None))
    return jax.shard_map(
        on_device,
        mesh=mesh,
        in_specs=placed,
        out_specs=(P(None, None, "dp", "fsdp"), P("rep", "fsdp", None, "dp", None)),
        check_vma=False,
    )
```

```python
import functools

import jax
import jax.numpy as jnp
from jax import lax
from jax.experimental import pallas as pl
from jax.experimental.pallas import tpu as pltpu
from jax.sharding import PartitionSpec as P

MESH = pl.DeviceIdType.MESH
LANES = 128


def kernel(
    count, group, subgroups, width, blocks,
    probes_hbm, gate_hbm, up_hbm, owner_hbm, seeds_hbm,
    digest_ref, hidden_ref,
    owner_ref, seeds_ref, x_flat, x, gate, up, stage, got, part, part_in, total, plane_out, plane_in, dig_out, dig_in, dig_mine, dig_theirs,
    x_load, load_sem, x_send, x_recv, p_send, p_recv, z_send, z_recv, d_send, d_recv, e_sem,
):
    planes = count // group
    rows = x.shape[1]
    local_rows = gate.shape[0]
    nb = local_rows // LANES
    ranks = dig_out.shape[0]
    dig_rows = dig_out.shape[1]
    me = lax.axis_index("fsdp")
    plane, spot = me // group, me % group
    replica = lax.axis_index("rep")
    side = replica % 2
    other_replica = {"rep": replica + 1 - 2 * side}

    def peer(index):
        return {"fsdp": index}

    def remote(src, dst, send, recv, index):
        return pltpu.make_async_remote_copy(
            src_ref=src, dst_ref=dst, send_sem=send, recv_sem=recv,
            device_id=peer(index), device_id_type=MESH,
        )

    barrier = pltpu.get_barrier_semaphore()

    def greet(step, carry):
        pl.semaphore_signal(
            barrier, inc=1, device_id=peer((me + step) % count), device_id_type=MESH
        )
        return carry

    load_owner = pltpu.make_async_copy(owner_hbm, owner_ref, load_sem.at[2])
    load_seeds = pltpu.make_async_copy(seeds_hbm, seeds_ref, load_sem.at[3])
    load_gate = pltpu.make_async_copy(gate_hbm, gate, load_sem.at[0])
    load_up = pltpu.make_async_copy(up_hbm, up, load_sem.at[1])
    quarter = blocks // 4
    loads = []
    for c in range(4):
        columns = pl.ds(c * quarter * LANES, quarter * LANES)
        loads.append(
            pltpu.make_async_copy(probes_hbm.at[:, columns], x_flat.at[:, columns], x_load.at[c])
        )
    load_owner.start()
    for load in loads:
        load.start()
    lax.fori_loop(1, count, greet, 0)
    pl.semaphore_signal(barrier, inc=1, device_id=other_replica, device_id_type=MESH)
    load_gate.start()
    load_up.start()
    load_seeds.start()
    for c in range(4):
        loads[c].wait()
        for block in range(c * quarter, (c + 1) * quarter):
            x[block] = x_flat[:, block * LANES : (block + 1) * LANES]
    load_owner.wait()

    def pick(target, into):
        for i in range(nb):
            block = owner_ref[target * nb + i]
            into[target, :, i * LANES : (i + 1) * LANES] = x[block]


    def rows_of(half):
        return pl.ds(0, rows)

    def slot(index, half):
        return index

    def halves(m):
        return (None,)

    def x_copy(target, half=None):
        return remote(
            stage.at[target, rows_of(half)], got.at[me, rows_of(half)],
            x_send.at[slot(target, half)], x_recv.at[slot(me, half)], target,
        )

    def x_arrival(source, half=None):
        return remote(
            stage.at[source, rows_of(half)], got.at[source, rows_of(half)],
            x_send.at[slot(source, half)], x_recv.at[slot(source, half)], source,
        )

    pl.semaphore_wait(barrier, count)
    def partner(m):
        other = plane * 0
        for bit in range((planes - 1).bit_length()):
            digit = (plane // 2**bit) % 2
            other = other + 2**bit * (1 - digit if (m >> bit) & 1 else digit)
        return other

    def target_of(m, j):
        return partner(m) * group + (spot + j) % group

    def send(m, j, half=None):
        if half != 1:
            pick(target_of(m, j), stage)
        x_copy(target_of(m, j), half).start()

    def send_phase(m, last, half=None):
        def one(j, carry):
            send(m, j, half)
            return carry

        lax.fori_loop(1, last, one, 0)

    send_phase(2, group + 1)
    send_phase(0, group)
    send_phase(1, group + 1)

    @pl.when(spot % 2 == 0)
    def _():
        send_phase(3, group + 1)

    pick(me, got)

    def squares(block, acc):
        wide = x[block].astype(jnp.float32)
        return acc + wide * wide

    acc = lax.fori_loop(0, blocks, squares, jnp.zeros((rows, LANES), jnp.float32))
    meansq = jnp.sum(acc, axis=1, keepdims=True) / (blocks * LANES)
    scale = 1.0 / jnp.sqrt(meansq + 1e-05)

    load_seeds.wait()
    row_id = lax.broadcasted_iota(jnp.int32, (16, LANES), 0)
    for_left, for_right = [], []
    for i in range(nb):
        held = lax.broadcasted_iota(jnp.int32, seeds_ref.shape, 0) == owner_ref[me * nb + i]
        seeds = jnp.sum(jnp.where(held, seeds_ref[...], 0), axis=0, keepdims=True)
        signs = jnp.broadcast_to(8 * (1 - 2 * seeds), (16, LANES)).astype(jnp.float32)
        for_left.append(jnp.where(row_id == i, signs, 0.0))
        for_right.append(jnp.where(row_id == nb + i, signs, 0.0))
    for_left = jnp.concatenate(for_left, axis=1).astype(jnp.bfloat16)
    for_right = jnp.concatenate(for_right, axis=1).astype(jnp.bfloat16)
    load_gate.wait()
    load_up.wait()

    def columns_of(t):
        return pl.ds(pl.multiple_of(t * width, width), width)

    half_width = width // 2

    def sketch_all(weights):
        def sketch(t, carry):
            left = pl.ds(pl.multiple_of(t * width, width), half_width)
            right = pl.ds(pl.multiple_of(t * width + half_width, half_width), half_width)
            both = jnp.dot(for_left, weights[:, left], preferred_element_type=jnp.float32)
            both += jnp.dot(for_right, weights[:, right], preferred_element_type=jnp.float32)
            dig_out[t] = both[:dig_rows]
            return carry

        lax.fori_loop(0, ranks, sketch, 0)

    @pl.when(side == 0)
    def _():
        sketch_all(gate)

    @pl.when(side == 1)
    def _():
        sketch_all(up)

    dig_in[me] = dig_out[me // subgroups]

    def d_copy(target):
        return remote(
            dig_out.at[target // subgroups], dig_in.at[me], d_send.at[target], d_recv.at[me], target
        )

    def d_arrival(source):
        return remote(
            dig_out.at[source // subgroups], dig_in.at[source], d_send.at[source],
            d_recv.at[source], source,
        )

    def send_digest(step, carry):
        d_copy((me + step) % count).start()
        return carry

    lax.fori_loop(1, count, send_digest, 0)

    def product(source, half=None):
        rows_in = got[source, rows_of(half)]
        columns = columns_of(source // subgroups)
        return (
            jnp.dot(rows_in, gate[:, columns], preferred_element_type=jnp.float32),
            jnp.dot(rows_in, up[:, columns], preferred_element_type=jnp.float32),
        )

    def p_copy(source_plane, spot_to, half=None):
        index, here = source_plane * group + spot_to, source_plane * group + spot
        return remote(
            part.at[index, rows_of(half)], part_in.at[here, rows_of(half)],
            p_send.at[slot(index, half)], p_recv.at[slot(here, half)],
            plane * group + spot_to,
        )

    def p_arrival(source_plane, spot_from, half=None):
        index = source_plane * group + spot_from
        return remote(
            part.at[index, rows_of(half)], part_in.at[index, rows_of(half)],
            p_send.at[slot(index, half)], p_recv.at[slot(index, half)],
            plane * group + spot_from,
        )

    def z_copy(m, half=None):
        index = m + planes if half == 1 else m
        return remote(
            plane_out.at[m, rows_of(half)], plane_in.at[m, rows_of(half)],
            z_send.at[index], z_recv.at[index],
            partner(m if m % 2 else 1) * group + spot,
        )

    def multiply_other(m, spot_from, half=None):
        source = partner(m) * group + spot_from
        a, b = product(source, half)
        part[source, rows_of(half), :width] = a.astype(jnp.bfloat16)
        part[source, rows_of(half), width:] = b.astype(jnp.bfloat16)
        p_copy(partner(m), spot_from, half).start()

    def multiply_own(m, half=None):
        a, b = product(partner(m) * group + spot, half)
        total[m, rows_of(half), :width] = a
        total[m, rows_of(half), width:] = b

    def start_following(m, j):
        if m >= 2 and m + 1 < planes:
            if m % 2:
                send(m + 1, j)
                return
            turn = (1 - spot % 2) * 2 if m == 2 else spot % 2

            @pl.when((j - 1) // 2 == turn)
            def _():
                send(m + 1, 2 * ((j - 1) % 2) + 1)
                send(m + 1, 2 * ((j - 1) % 2) + 2)

    def multiply(m):
        def others(j, carry):
            spot_from = (spot + group - j) % group
            x_arrival(partner(m) * group + spot_from).wait_recv()
            start_following(m, j)
            multiply_other(m, spot_from)
            return carry

        lax.fori_loop(1, group, others, 0)
        if m != 0:
            x_arrival(partner(m) * group + spot).wait_recv()
            start_following(m, group)
        multiply_own(m)

    def multiply_staggered(m):
        for odd in range(2):
            for half in halves(m):
                def one(step, carry, odd=odd, half=half):
                    j = 2 - (spot + odd) % 2 + 2 * step
                    spot_from = (spot + group - j) % group
                    x_arrival(partner(m) * group + spot_from, half).wait_recv()
                    start_following(m, 2 * odd + step + 1)

                    @pl.when(j == group)
                    def _():
                        multiply_own(m, half)

                    @pl.when(j != group)
                    def _():
                        multiply_other(m, spot_from, half)

                    return carry

                lax.fori_loop(0, 2, one, 0)

                @pl.when(spot % 2 == odd)
                def _():
                    reduce(m, half)

    def reduce(m, half=None):
        summed = total[m, rows_of(half)]
        if m > 2 and m % 2:
            z_copy(m - 1).wait_recv()
            summed += plane_in[m - 1, rows_of(half)].astype(jnp.float32)
        for j in range(1, group):
            p_arrival(partner(m), (spot + group - j) % group, half).wait_recv()
        for j in range(1, group):
            index = partner(m) * group + (spot + group - j) % group
            summed += part_in[index, rows_of(half)].astype(jnp.float32)
        if m > 0:
            plane_out[m, rows_of(half)] = summed.astype(jnp.bfloat16)
            z_copy(m, half).start()
        else:
            total[m] = summed

    multiply(0)
    multiply(2)
    reduce(0)
    multiply(1)
    reduce(2)
    reduce(1)
    def wait_digest(step, carry):
        d_arrival((me + step) % count).wait_recv()
        return carry

    lax.fori_loop(1, count, wait_digest, 0)
    span = count * dig_rows
    column = lax.broadcasted_iota(jnp.int32, (8, span), 1)
    inner = column % dig_rows
    place = jnp.where(inner < 2 * nb, (column // dig_rows) * nb + inner % nb, -1)
    owners = jnp.full((8, span), -1, jnp.int32)
    for j in range(blocks):
        owners = jnp.where(place == j, owner_ref[j], owners)
    owners = owners + jnp.where(inner >= nb, blocks, 0)
    owners = jnp.where(inner < 2 * nb, owners, -1)
    wanted = lax.broadcasted_iota(jnp.int32, (2 * blocks, span), 0)
    chosen = jnp.where(jnp.broadcast_to(owners[:1], (2 * blocks, span)) == wanted, 1.0, 0.0)
    ordered = jnp.dot(
        chosen, dig_in[...].reshape(span, half_width),
        precision=lax.Precision.HIGHEST, preferred_element_type=jnp.float32,
    )
    dig_mine[:, :half_width] = ordered[:blocks]
    dig_mine[:, half_width:] = ordered[blocks:]
    exchange = pltpu.make_async_remote_copy(
        src_ref=dig_mine, dst_ref=dig_theirs, send_sem=e_sem.at[0], recv_sem=e_sem.at[1],
        device_id=other_replica, device_id_type=MESH,
    )
    exchange.start()

    for m in range(3, planes):
        if m % 2:
            multiply_staggered(m)
        else:
            multiply(m)
            reduce(m)

    digest_ref[pl.ds(pl.multiple_of(side * blocks, blocks), blocks), :] = dig_mine[...]
    exchange.wait()
    digest_ref[pl.ds(pl.multiple_of((1 - side) * blocks, blocks), blocks), :] = dig_theirs[...]

    def drain_digest(step, carry):
        d_copy((me + step) % count).wait_send()
        return carry

    lax.fori_loop(1, count, drain_digest, 0)
    for m in range(planes):
        for half in halves(m):
            def drain_spot(j, carry, m=m, half=half):
                x_copy(target_of(m, j), half).wait_send()
                return carry

            def drain_part(j, carry, m=m, half=half):
                p_copy(partner(m), (spot + group - j) % group, half).wait_send()
                return carry

            lax.fori_loop(1, group + (m > 0), drain_spot, 0)
            lax.fori_loop(1, group, drain_part, 0)

    summed = total[0]
    for m in range(1, planes, 2):
        z_copy(m).wait_recv()
        summed += plane_in[m].astype(jnp.float32)
    gate_sum = summed[:, :width] * scale
    up_sum = summed[:, width:] * scale
    hidden_ref[...] = (gate_sum / (1.0 + jnp.exp(-gate_sum)) * up_sum).astype(jnp.bfloat16)

    for m in range(1, planes):
        for half in halves(m):
            z_copy(m, half).wait_send()


def on_device(trainer_gate, trainer_up, owner_map, sketch_seeds, probes):
    local_rows, _, slice_width = trainer_gate.shape
    count = lax.axis_size("fsdp")
    ranks = min(16, count)
    subgroups = count // ranks
    width = slice_width // ranks
    narrow = width // subgroups
    group = 4
    planes = count // group
    total_rows = local_rows * count
    blocks = total_rows // LANES
    nb = local_rows // LANES
    dig_rows = -(-2 * nb // 8) * 8
    rows = probes.shape[2]
    bf16, f32 = jnp.bfloat16, jnp.float32
    dma = pltpu.SemaphoreType.DMA
    digest, hidden = pl.pallas_call(
        functools.partial(kernel, count, group, subgroups, width, blocks),
        out_shape=(
            pltpu.VMEM((2 * blocks, width), f32),
            pltpu.VMEM((rows, width), bf16),
        ),
        in_specs=[pl.BlockSpec(memory_space=pl.ANY)] * 5,
        out_specs=[pl.BlockSpec(memory_space=pltpu.VMEM)] * 2,
        scratch_shapes=[
            pltpu.SMEM((blocks,), jnp.int32),
            pltpu.VMEM((blocks, LANES), jnp.int32),
            pltpu.VMEM((rows, total_rows), bf16),
            pltpu.VMEM((blocks, rows, LANES), bf16),
            pltpu.VMEM((local_rows, slice_width), bf16),
            pltpu.VMEM((local_rows, slice_width), bf16),
            pltpu.VMEM((count, rows, local_rows), bf16),
            pltpu.VMEM((count, rows, local_rows), bf16),
            pltpu.VMEM((count, rows, 2 * width), bf16),
            pltpu.VMEM((count, rows, 2 * width), bf16),
            pltpu.VMEM((planes, rows, 2 * width), f32),
            pltpu.VMEM((planes, rows, 2 * width), bf16),
            pltpu.VMEM((planes, rows, 2 * width), bf16),
            pltpu.VMEM((ranks, dig_rows, width // 2), f32),
            pltpu.VMEM((count, dig_rows, width // 2), f32),
            pltpu.VMEM((blocks, width), f32),
            pltpu.VMEM((blocks, width), f32),
            dma((4,)), dma((4,)),
            dma((2 * count,)), dma((2 * count,)),
            dma((2 * count,)), dma((2 * count,)),
            dma((2 * planes,)), dma((2 * planes,)),
            dma((count,)), dma((count,)),
            dma((2,)),
        ],
        compiler_params=pltpu.CompilerParams(
            collective_id=0, has_side_effects=True, vmem_limit_bytes=60 * 2**20
        ),
    )(
        probes.reshape(rows, total_rows),
        trainer_gate.reshape(local_rows, slice_width),
        trainer_up.reshape(local_rows, slice_width),
        owner_map,
        sketch_seeds.reshape(blocks, LANES),
    )
    if subgroups > 1:
        member = lax.axis_index("fsdp")
        digest = lax.dynamic_slice_in_dim(digest, (member % subgroups) * narrow, narrow, 1)
    return (
        digest.reshape(2, blocks, 1, narrow),
        hidden.reshape(1, 1, rows, 1, width),
    )


def solution(mesh):
    placed = (P("fsdp", "dp", None), P("fsdp", "dp", None), P(), P(), P("rep", "fsdp", None, None))
    return jax.shard_map(
        on_device,
        mesh=mesh,
        in_specs=placed,
        out_specs=(P(None, None, "dp", "fsdp"), P("rep", "fsdp", None, "dp", None)),
        check_vma=False,
    )
```

```python
import functools

import jax
import jax.numpy as jnp
from jax import lax
from jax.experimental import pallas as pl
from jax.experimental.pallas import tpu as pltpu
from jax.sharding import PartitionSpec as P

MESH = pl.DeviceIdType.MESH
LANES = 128


def kernel(
    count, group, subgroups, width, blocks,
    probes_hbm, gate_hbm, up_hbm, owner_hbm, seeds_hbm,
    digest_ref, hidden_ref,
    owner_ref, seeds_ref, x_flat, x, gate, up, stage, got, part, part_in, total, plane_out, plane_in, dig_out, dig_in, dig_mine, dig_theirs,
    x_load, load_sem, x_send, x_recv, p_send, p_recv, z_send, z_recv, d_send, d_recv, e_sem,
):
    planes = count // group
    rows = x.shape[1]
    local_rows = gate.shape[0]
    nb = local_rows // LANES
    ranks = dig_out.shape[0]
    dig_rows = dig_out.shape[1]
    me = lax.axis_index("fsdp")
    plane, spot = me // group, me % group
    replica = lax.axis_index("rep")
    side = replica % 2
    other_replica = {"rep": replica + 1 - 2 * side}

    def peer(index):
        return {"fsdp": index}

    def remote(src, dst, send, recv, index):
        return pltpu.make_async_remote_copy(
            src_ref=src, dst_ref=dst, send_sem=send, recv_sem=recv,
            device_id=peer(index), device_id_type=MESH,
        )

    barrier = pltpu.get_barrier_semaphore()

    def greet(step, carry):
        pl.semaphore_signal(
            barrier, inc=1, device_id=peer((me + step) % count), device_id_type=MESH
        )
        return carry

    load_owner = pltpu.make_async_copy(owner_hbm, owner_ref, load_sem.at[2])
    load_seeds = pltpu.make_async_copy(seeds_hbm, seeds_ref, load_sem.at[3])
    load_gate = pltpu.make_async_copy(gate_hbm, gate, load_sem.at[0])
    load_up = pltpu.make_async_copy(up_hbm, up, load_sem.at[1])
    quarter = blocks // 4
    loads = []
    for c in range(4):
        columns = pl.ds(c * quarter * LANES, quarter * LANES)
        loads.append(
            pltpu.make_async_copy(probes_hbm.at[:, columns], x_flat.at[:, columns], x_load.at[c])
        )
    load_owner.start()
    for load in loads:
        load.start()
    lax.fori_loop(1, count, greet, 0)
    pl.semaphore_signal(barrier, inc=1, device_id=other_replica, device_id_type=MESH)
    load_gate.start()
    load_up.start()
    load_seeds.start()
    for c in range(4):
        loads[c].wait()
        for block in range(c * quarter, (c + 1) * quarter):
            x[block] = x_flat[:, block * LANES : (block + 1) * LANES]
    load_owner.wait()

    def pick(target, into):
        for i in range(nb):
            block = owner_ref[target * nb + i]
            into[target, :, i * LANES : (i + 1) * LANES] = x[block]


    def rows_of(half):
        return pl.ds(0, rows)

    def slot(index, half):
        return index

    def halves(m):
        return (None,)

    def x_copy(target, half=None):
        return remote(
            stage.at[target, rows_of(half)], got.at[me, rows_of(half)],
            x_send.at[slot(target, half)], x_recv.at[slot(me, half)], target,
        )

    def x_arrival(source, half=None):
        return remote(
            stage.at[source, rows_of(half)], got.at[source, rows_of(half)],
            x_send.at[slot(source, half)], x_recv.at[slot(source, half)], source,
        )

    pl.semaphore_wait(barrier, count)
    def partner(m):
        other = plane * 0
        for bit in range((planes - 1).bit_length()):
            digit = (plane // 2**bit) % 2
            other = other + 2**bit * (1 - digit if (m >> bit) & 1 else digit)
        return other

    def target_of(m, j):
        return partner(m) * group + (spot + j) % group

    def send(m, j, half=None):
        if half != 1:
            pick(target_of(m, j), stage)
        x_copy(target_of(m, j), half).start()

    def send_phase(m, last, half=None):
        def one(j, carry):
            send(m, j, half)
            return carry

        lax.fori_loop(1, last, one, 0)

    send_phase(2, group + 1)
    send_phase(0, group)
    send_phase(1, group + 1)

    @pl.when(spot % 2 == 0)
    def _():
        send_phase(3, group + 1)

    pick(me, got)

    def squares(block, acc):
        wide = x[block].astype(jnp.float32)
        return acc + wide * wide

    acc = lax.fori_loop(0, blocks, squares, jnp.zeros((rows, LANES), jnp.float32))
    meansq = jnp.sum(acc, axis=1, keepdims=True) / (blocks * LANES)
    scale = 1.0 / jnp.sqrt(meansq + 1e-05)

    load_seeds.wait()
    row_id = lax.broadcasted_iota(jnp.int32, (16, LANES), 0)
    for_left, for_right = [], []
    for i in range(nb):
        held = lax.broadcasted_iota(jnp.int32, seeds_ref.shape, 0) == owner_ref[me * nb + i]
        seeds = jnp.sum(jnp.where(held, seeds_ref[...], 0), axis=0, keepdims=True)
        signs = jnp.broadcast_to(8 * (1 - 2 * seeds), (16, LANES)).astype(jnp.float32)
        for_left.append(jnp.where(row_id == i, signs, 0.0))
        for_right.append(jnp.where(row_id == nb + i, signs, 0.0))
    for_left = jnp.concatenate(for_left, axis=1).astype(jnp.bfloat16)
    for_right = jnp.concatenate(for_right, axis=1).astype(jnp.bfloat16)
    load_gate.wait()
    load_up.wait()

    def columns_of(t):
        return pl.ds(pl.multiple_of(t * width, width), width)

    half_width = width // 2

    def sketch_all(weights):
        def sketch(t, carry):
            left = pl.ds(pl.multiple_of(t * width, width), half_width)
            right = pl.ds(pl.multiple_of(t * width + half_width, half_width), half_width)
            both = jnp.dot(for_left, weights[:, left], preferred_element_type=jnp.float32)
            both += jnp.dot(for_right, weights[:, right], preferred_element_type=jnp.float32)
            dig_out[t] = both[:dig_rows]
            return carry

        lax.fori_loop(0, ranks, sketch, 0)

    @pl.when(side == 0)
    def _():
        sketch_all(gate)

    @pl.when(side == 1)
    def _():
        sketch_all(up)

    dig_in[me] = dig_out[me // subgroups]

    def d_copy(target):
        return remote(
            dig_out.at[target // subgroups], dig_in.at[me], d_send.at[target], d_recv.at[me], target
        )

    def d_arrival(source):
        return remote(
            dig_out.at[source // subgroups], dig_in.at[source], d_send.at[source],
            d_recv.at[source], source,
        )

    def send_digest(step, carry):
        d_copy((me + step) % count).start()
        return carry

    lax.fori_loop(1, count, send_digest, 0)

    def product(source, half=None):
        rows_in = got[source, rows_of(half)]
        columns = columns_of(source // subgroups)
        return (
            jnp.dot(rows_in, gate[:, columns], preferred_element_type=jnp.float32),
            jnp.dot(rows_in, up[:, columns], preferred_element_type=jnp.float32),
        )

    def p_copy(source_plane, spot_to, half=None):
        index, here = source_plane * group + spot_to, source_plane * group + spot
        return remote(
            part.at[index, rows_of(half)], part_in.at[here, rows_of(half)],
            p_send.at[slot(index, half)], p_recv.at[slot(here, half)],
            plane * group + spot_to,
        )

    def p_arrival(source_plane, spot_from, half=None):
        index = source_plane * group + spot_from
        return remote(
            part.at[index, rows_of(half)], part_in.at[index, rows_of(half)],
            p_send.at[slot(index, half)], p_recv.at[slot(index, half)],
            plane * group + spot_from,
        )

    def z_copy(m, half=None):
        index = m + planes if half == 1 else m
        return remote(
            plane_out.at[m, rows_of(half)], plane_in.at[m, rows_of(half)],
            z_send.at[index], z_recv.at[index],
            partner(m if m % 2 else 1) * group + spot,
        )

    def multiply_other(m, spot_from, half=None):
        source = partner(m) * group + spot_from
        a, b = product(source, half)
        part[source, rows_of(half), :width] = a.astype(jnp.bfloat16)
        part[source, rows_of(half), width:] = b.astype(jnp.bfloat16)
        p_copy(partner(m), spot_from, half).start()

    def multiply_own(m, half=None):
        a, b = product(partner(m) * group + spot, half)
        total[m, rows_of(half), :width] = a
        total[m, rows_of(half), width:] = b

    def start_following(m, j):
        if m >= 2 and m + 1 < planes:
            if m % 2:
                send(m + 1, j)
                return
            turn = (1 - spot % 2) * 2 if m == 2 else spot % 2

            @pl.when((j - 1) // 2 == turn)
            def _():
                send(m + 1, 2 * ((j - 1) % 2) + 1)
                send(m + 1, 2 * ((j - 1) % 2) + 2)

    def multiply(m):
        def others(j, carry):
            spot_from = (spot + group - j) % group
            x_arrival(partner(m) * group + spot_from).wait_recv()
            start_following(m, j)
            multiply_other(m, spot_from)
            return carry

        lax.fori_loop(1, group, others, 0)
        if m != 0:
            x_arrival(partner(m) * group + spot).wait_recv()
            start_following(m, group)
        multiply_own(m)

    def multiply_staggered(m):
        for odd in range(2):
            for half in halves(m):
                def one(step, carry, odd=odd, half=half):
                    j = 2 - (spot + odd) % 2 + 2 * step
                    spot_from = (spot + group - j) % group
                    x_arrival(partner(m) * group + spot_from, half).wait_recv()
                    start_following(m, 2 * odd + step + 1)

                    @pl.when(j == group)
                    def _():
                        multiply_own(m, half)

                    @pl.when(j != group)
                    def _():
                        multiply_other(m, spot_from, half)

                    return carry

                lax.fori_loop(0, 2, one, 0)

                @pl.when(spot % 2 == odd)
                def _():
                    reduce(m, half)

    def reduce(m, half=None):
        summed = total[m, rows_of(half)]
        if m > 2 and m % 2:
            z_copy(m - 1).wait_recv()
            summed += plane_in[m - 1, rows_of(half)].astype(jnp.float32)
        for j in range(1, group):
            p_arrival(partner(m), (spot + group - j) % group, half).wait_recv()
        for j in range(1, group):
            index = partner(m) * group + (spot + group - j) % group
            summed += part_in[index, rows_of(half)].astype(jnp.float32)
        if m > 0:
            plane_out[m, rows_of(half)] = summed.astype(jnp.bfloat16)
            z_copy(m, half).start()
        else:
            total[m] = summed

    multiply(0)
    multiply(2)
    reduce(0)
    multiply(1)
    reduce(2)
    reduce(1)
    for m in range(3, planes):
        if m % 2:
            multiply_staggered(m)
        else:
            multiply(m)
            reduce(m)

    def wait_digest(step, carry):
        d_arrival((me + step) % count).wait_recv()
        return carry

    lax.fori_loop(1, count, wait_digest, 0)
    span = count * dig_rows
    column = lax.broadcasted_iota(jnp.int32, (8, span), 1)
    inner = column % dig_rows
    place = jnp.where(inner < 2 * nb, (column // dig_rows) * nb + inner % nb, -1)
    owners = jnp.full((8, span), -1, jnp.int32)
    for j in range(blocks):
        owners = jnp.where(place == j, owner_ref[j], owners)
    owners = owners + jnp.where(inner >= nb, blocks, 0)
    owners = jnp.where(inner < 2 * nb, owners, -1)
    wanted = lax.broadcasted_iota(jnp.int32, (2 * blocks, span), 0)
    chosen = jnp.where(jnp.broadcast_to(owners[:1], (2 * blocks, span)) == wanted, 1.0, 0.0)
    ordered = jnp.dot(
        chosen, dig_in[...].reshape(span, half_width),
        precision=lax.Precision.HIGHEST, preferred_element_type=jnp.float32,
    )
    dig_mine[:, :half_width] = ordered[:blocks]
    dig_mine[:, half_width:] = ordered[blocks:]
    exchange = pltpu.make_async_remote_copy(
        src_ref=dig_mine, dst_ref=dig_theirs, send_sem=e_sem.at[0], recv_sem=e_sem.at[1],
        device_id=other_replica, device_id_type=MESH,
    )
    exchange.start()

    def drain_digest(step, carry):
        d_copy((me + step) % count).wait_send()
        return carry

    lax.fori_loop(1, count, drain_digest, 0)
    for m in range(planes):
        for half in halves(m):
            def drain_spot(j, carry, m=m, half=half):
                x_copy(target_of(m, j), half).wait_send()
                return carry

            def drain_part(j, carry, m=m, half=half):
                p_copy(partner(m), (spot + group - j) % group, half).wait_send()
                return carry

            lax.fori_loop(1, group + (m > 0), drain_spot, 0)
            lax.fori_loop(1, group, drain_part, 0)

    digest_ref[pl.ds(pl.multiple_of(side * blocks, blocks), blocks), :] = dig_mine[...]
    exchange.wait()
    digest_ref[pl.ds(pl.multiple_of((1 - side) * blocks, blocks), blocks), :] = dig_theirs[...]

    summed = total[0]
    for m in range(1, planes, 2):
        z_copy(m).wait_recv()
        summed += plane_in[m].astype(jnp.float32)
    gate_sum = summed[:, :width] * scale
    up_sum = summed[:, width:] * scale
    hidden_ref[...] = (gate_sum / (1.0 + jnp.exp(-gate_sum)) * up_sum).astype(jnp.bfloat16)

    for m in range(1, planes):
        for half in halves(m):
            z_copy(m, half).wait_send()


def on_device(trainer_gate, trainer_up, owner_map, sketch_seeds, probes):
    local_rows, _, slice_width = trainer_gate.shape
    count = lax.axis_size("fsdp")
    ranks = min(16, count)
    subgroups = count // ranks
    width = slice_width // ranks
    narrow = width // subgroups
    group = 4
    planes = count // group
    total_rows = local_rows * count
    blocks = total_rows // LANES
    nb = local_rows // LANES
    dig_rows = -(-2 * nb // 8) * 8
    rows = probes.shape[2]
    bf16, f32 = jnp.bfloat16, jnp.float32
    dma = pltpu.SemaphoreType.DMA
    digest, hidden = pl.pallas_call(
        functools.partial(kernel, count, group, subgroups, width, blocks),
        out_shape=(
            pltpu.VMEM((2 * blocks, width), f32),
            pltpu.VMEM((rows, width), bf16),
        ),
        in_specs=[pl.BlockSpec(memory_space=pl.ANY)] * 5,
        out_specs=[pl.BlockSpec(memory_space=pltpu.VMEM)] * 2,
        scratch_shapes=[
            pltpu.SMEM((blocks,), jnp.int32),
            pltpu.VMEM((blocks, LANES), jnp.int32),
            pltpu.VMEM((rows, total_rows), bf16),
            pltpu.VMEM((blocks, rows, LANES), bf16),
            pltpu.VMEM((local_rows, slice_width), bf16),
            pltpu.VMEM((local_rows, slice_width), bf16),
            pltpu.VMEM((count, rows, local_rows), bf16),
            pltpu.VMEM((count, rows, local_rows), bf16),
            pltpu.VMEM((count, rows, 2 * width), bf16),
            pltpu.VMEM((count, rows, 2 * width), bf16),
            pltpu.VMEM((planes, rows, 2 * width), f32),
            pltpu.VMEM((planes, rows, 2 * width), bf16),
            pltpu.VMEM((planes, rows, 2 * width), bf16),
            pltpu.VMEM((ranks, dig_rows, width // 2), f32),
            pltpu.VMEM((count, dig_rows, width // 2), f32),
            pltpu.VMEM((blocks, width), f32),
            pltpu.VMEM((blocks, width), f32),
            dma((4,)), dma((4,)),
            dma((2 * count,)), dma((2 * count,)),
            dma((2 * count,)), dma((2 * count,)),
            dma((2 * planes,)), dma((2 * planes,)),
            dma((count,)), dma((count,)),
            dma((2,)),
        ],
        compiler_params=pltpu.CompilerParams(
            collective_id=0, has_side_effects=True, vmem_limit_bytes=60 * 2**20
        ),
    )(
        probes.reshape(rows, total_rows),
        trainer_gate.reshape(local_rows, slice_width),
        trainer_up.reshape(local_rows, slice_width),
        owner_map,
        sketch_seeds.reshape(blocks, LANES),
    )
    if subgroups > 1:
        member = lax.axis_index("fsdp")
        digest = lax.dynamic_slice_in_dim(digest, (member % subgroups) * narrow, narrow, 1)
    return (
        digest.reshape(2, blocks, 1, narrow),
        hidden.reshape(1, 1, rows, 1, width),
    )


def solution(mesh):
    placed = (P("fsdp", "dp", None), P("fsdp", "dp", None), P(), P(), P("rep", "fsdp", None, None))
    return jax.shard_map(
        on_device,
        mesh=mesh,
        in_specs=placed,
        out_specs=(P(None, None, "dp", "fsdp"), P("rep", "fsdp", None, "dp", None)),
        check_vma=False,
    )
```

```python
import functools

import jax
import jax.numpy as jnp
from jax import lax
from jax.experimental import pallas as pl
from jax.experimental.pallas import tpu as pltpu
from jax.sharding import PartitionSpec as P

MESH = pl.DeviceIdType.MESH
LANES = 128


def kernel(
    count, group, subgroups, width, blocks,
    probes_hbm, gate_hbm, up_hbm, owner_hbm, seeds_hbm,
    digest_ref, hidden_ref,
    owner_ref, seeds_ref, x_flat, x, gate, up, stage, got, part, part_in, total, plane_out, plane_in, dig_out, dig_in, dig_mine, dig_theirs,
    x_load, load_sem, x_send, x_recv, p_send, p_recv, z_send, z_recv, d_send, d_recv, e_sem,
):
    planes = count // group
    rows = x.shape[1]
    local_rows = gate.shape[0]
    nb = local_rows // LANES
    ranks = dig_out.shape[0]
    dig_rows = dig_out.shape[1]
    me = lax.axis_index("fsdp")
    plane, spot = me // group, me % group
    replica = lax.axis_index("rep")
    side = replica % 2
    other_replica = {"rep": replica + 1 - 2 * side}

    def peer(index):
        return {"fsdp": index}

    def remote(src, dst, send, recv, index):
        return pltpu.make_async_remote_copy(
            src_ref=src, dst_ref=dst, send_sem=send, recv_sem=recv,
            device_id=peer(index), device_id_type=MESH,
        )

    barrier = pltpu.get_barrier_semaphore()

    def greet(step, carry):
        pl.semaphore_signal(
            barrier, inc=1, device_id=peer((me + step) % count), device_id_type=MESH
        )
        return carry

    load_owner = pltpu.make_async_copy(owner_hbm, owner_ref, load_sem.at[2])
    load_seeds = pltpu.make_async_copy(seeds_hbm, seeds_ref, load_sem.at[3])
    load_gate = pltpu.make_async_copy(gate_hbm, gate, load_sem.at[0])
    load_up = pltpu.make_async_copy(up_hbm, up, load_sem.at[1])
    quarter = blocks // 4
    loads = []
    for c in range(4):
        columns = pl.ds(c * quarter * LANES, quarter * LANES)
        loads.append(
            pltpu.make_async_copy(probes_hbm.at[:, columns], x_flat.at[:, columns], x_load.at[c])
        )
    load_owner.start()
    for load in loads:
        load.start()
    lax.fori_loop(1, count, greet, 0)
    pl.semaphore_signal(barrier, inc=1, device_id=other_replica, device_id_type=MESH)
    load_gate.start()
    load_up.start()
    load_seeds.start()
    for c in range(4):
        loads[c].wait()
        for block in range(c * quarter, (c + 1) * quarter):
            x[block] = x_flat[:, block * LANES : (block + 1) * LANES]
    load_owner.wait()

    def pick(target, into):
        for i in range(nb):
            block = owner_ref[target * nb + i]
            into[target, :, i * LANES : (i + 1) * LANES] = x[block]


    def rows_of(half):
        return pl.ds(0, rows)

    def slot(index, half):
        return index

    def halves(m):
        return (None,)

    def x_copy(target, half=None):
        return remote(
            stage.at[target, rows_of(half)], got.at[me, rows_of(half)],
            x_send.at[slot(target, half)], x_recv.at[slot(me, half)], target,
        )

    def x_arrival(source, half=None):
        return remote(
            stage.at[source, rows_of(half)], got.at[source, rows_of(half)],
            x_send.at[slot(source, half)], x_recv.at[slot(source, half)], source,
        )

    pl.semaphore_wait(barrier, count)
    def partner(m):
        other = plane * 0
        for bit in range((planes - 1).bit_length()):
            digit = (plane // 2**bit) % 2
            other = other + 2**bit * (1 - digit if (m >> bit) & 1 else digit)
        return other

    def target_of(m, j):
        return partner(m) * group + (spot + j) % group

    def send(m, j, half=None):
        if half != 1:
            pick(target_of(m, j), stage)
        x_copy(target_of(m, j), half).start()

    def send_phase(m, last, half=None):
        def one(j, carry):
            send(m, j, half)
            return carry

        lax.fori_loop(1, last, one, 0)

    send_phase(2, group + 1)
    send_phase(0, group)
    send_phase(1, group + 1)

    @pl.when(spot % 2 == 0)
    def _():
        send_phase(3, group + 1)

    pick(me, got)

    def squares(block, acc):
        wide = x[block].astype(jnp.float32)
        return acc + wide * wide

    acc = lax.fori_loop(0, blocks, squares, jnp.zeros((rows, LANES), jnp.float32))
    meansq = jnp.sum(acc, axis=1, keepdims=True) / (blocks * LANES)
    scale = 1.0 / jnp.sqrt(meansq + 1e-05)

    load_seeds.wait()
    row_id = lax.broadcasted_iota(jnp.int32, (16, LANES), 0)
    for_left, for_right = [], []
    for i in range(nb):
        held = lax.broadcasted_iota(jnp.int32, seeds_ref.shape, 0) == owner_ref[me * nb + i]
        seeds = jnp.sum(jnp.where(held, seeds_ref[...], 0), axis=0, keepdims=True)
        signs = jnp.broadcast_to(8 * (1 - 2 * seeds), (16, LANES)).astype(jnp.float32)
        for_left.append(jnp.where(row_id == i, signs, 0.0))
        for_right.append(jnp.where(row_id == nb + i, signs, 0.0))
    for_left = jnp.concatenate(for_left, axis=1).astype(jnp.bfloat16)
    for_right = jnp.concatenate(for_right, axis=1).astype(jnp.bfloat16)
    load_gate.wait()
    load_up.wait()

    def columns_of(t):
        return pl.ds(pl.multiple_of(t * width, width), width)

    half_width = width // 2

    def sketch_all(weights):
        def sketch(t, carry):
            left = pl.ds(pl.multiple_of(t * width, width), half_width)
            right = pl.ds(pl.multiple_of(t * width + half_width, half_width), half_width)
            both = jnp.dot(for_left, weights[:, left], preferred_element_type=jnp.float32)
            both += jnp.dot(for_right, weights[:, right], preferred_element_type=jnp.float32)
            dig_out[t] = both[:dig_rows]
            return carry

        lax.fori_loop(0, ranks, sketch, 0)

    @pl.when(side == 0)
    def _():
        sketch_all(gate)

    @pl.when(side == 1)
    def _():
        sketch_all(up)

    dig_in[me] = dig_out[me // subgroups]

    def d_copy(target):
        return remote(
            dig_out.at[target // subgroups], dig_in.at[me], d_send.at[target], d_recv.at[me], target
        )

    def d_arrival(source):
        return remote(
            dig_out.at[source // subgroups], dig_in.at[source], d_send.at[source],
            d_recv.at[source], source,
        )

    def send_digest(step, carry):
        d_copy((me + step) % count).start()
        return carry

    lax.fori_loop(1, count, send_digest, 0)

    def product(source, half=None):
        rows_in = got[source, rows_of(half)]
        columns = columns_of(source // subgroups)
        return (
            jnp.dot(rows_in, gate[:, columns], preferred_element_type=jnp.float32),
            jnp.dot(rows_in, up[:, columns], preferred_element_type=jnp.float32),
        )

    def p_copy(source_plane, spot_to, half=None):
        index, here = source_plane * group + spot_to, source_plane * group + spot
        return remote(
            part.at[index, rows_of(half)], part_in.at[here, rows_of(half)],
            p_send.at[slot(index, half)], p_recv.at[slot(here, half)],
            plane * group + spot_to,
        )

    def p_arrival(source_plane, spot_from, half=None):
        index = source_plane * group + spot_from
        return remote(
            part.at[index, rows_of(half)], part_in.at[index, rows_of(half)],
            p_send.at[slot(index, half)], p_recv.at[slot(index, half)],
            plane * group + spot_from,
        )

    def z_copy(m, half=None):
        index = m + planes if half == 1 else m
        return remote(
            plane_out.at[m, rows_of(half)], plane_in.at[m, rows_of(half)],
            z_send.at[index], z_recv.at[index],
            partner(m if m % 2 else 1) * group + spot,
        )

    def multiply_other(m, spot_from, half=None):
        source = partner(m) * group + spot_from
        a, b = product(source, half)
        part[source, rows_of(half), :width] = a.astype(jnp.bfloat16)
        part[source, rows_of(half), width:] = b.astype(jnp.bfloat16)
        p_copy(partner(m), spot_from, half).start()

    def multiply_own(m, half=None):
        a, b = product(partner(m) * group + spot, half)
        total[m, rows_of(half), :width] = a
        total[m, rows_of(half), width:] = b

    def start_following(m, j):
        if m >= 2 and m + 1 < planes:
            if m % 2:
                send(m + 1, j)
                return
            if m == 2:
                return

            @pl.when((j - 1) // 2 == spot % 2)
            def _():
                send(m + 1, 2 * ((j - 1) % 2) + 1)
                send(m + 1, 2 * ((j - 1) % 2) + 2)

    def multiply(m):
        def others(j, carry):
            spot_from = (spot + group - j) % group
            x_arrival(partner(m) * group + spot_from).wait_recv()
            start_following(m, j)
            multiply_other(m, spot_from)
            return carry

        lax.fori_loop(1, group, others, 0)
        if m != 0:
            x_arrival(partner(m) * group + spot).wait_recv()
            start_following(m, group)
        multiply_own(m)

    def multiply_staggered(m):
        for odd in range(2):
            for half in halves(m):
                def one(step, carry, odd=odd, half=half):
                    j = 2 - (spot + odd) % 2 + 2 * step
                    spot_from = (spot + group - j) % group
                    x_arrival(partner(m) * group + spot_from, half).wait_recv()
                    start_following(m, 2 * odd + step + 1)
                    if m == 3 and odd == 0:
                        @pl.when(spot % 2 == 1)
                        def _():
                            send(3, 2 * step + 1)
                            send(3, 2 * step + 2)


                    @pl.when(j == group)
                    def _():
                        multiply_own(m, half)

                    @pl.when(j != group)
                    def _():
                        multiply_other(m, spot_from, half)

                    return carry

                lax.fori_loop(0, 2, one, 0)

                @pl.when(spot % 2 == odd)
                def _():
                    reduce(m, half)

    def reduce(m, half=None):
        summed = total[m, rows_of(half)]
        if m > 2 and m % 2:
            z_copy(m - 1).wait_recv()
            summed += plane_in[m - 1, rows_of(half)].astype(jnp.float32)
        for j in range(1, group):
            p_arrival(partner(m), (spot + group - j) % group, half).wait_recv()
        for j in range(1, group):
            index = partner(m) * group + (spot + group - j) % group
            summed += part_in[index, rows_of(half)].astype(jnp.float32)
        if m > 0:
            plane_out[m, rows_of(half)] = summed.astype(jnp.bfloat16)
            z_copy(m, half).start()
        else:
            total[m] = summed

    multiply(0)
    multiply(2)
    reduce(0)
    multiply(1)
    reduce(2)
    reduce(1)
    for m in range(3, planes):
        if m % 2:
            multiply_staggered(m)
        else:
            multiply(m)
            reduce(m)

    def wait_digest(step, carry):
        d_arrival((me + step) % count).wait_recv()
        return carry

    lax.fori_loop(1, count, wait_digest, 0)
    span = count * dig_rows
    column = lax.broadcasted_iota(jnp.int32, (8, span), 1)
    inner = column % dig_rows
    place = jnp.where(inner < 2 * nb, (column // dig_rows) * nb + inner % nb, -1)
    owners = jnp.full((8, span), -1, jnp.int32)
    for j in range(blocks):
        owners = jnp.where(place == j, owner_ref[j], owners)
    owners = owners + jnp.where(inner >= nb, blocks, 0)
    owners = jnp.where(inner < 2 * nb, owners, -1)
    wanted = lax.broadcasted_iota(jnp.int32, (2 * blocks, span), 0)
    chosen = jnp.where(jnp.broadcast_to(owners[:1], (2 * blocks, span)) == wanted, 1.0, 0.0)
    ordered = jnp.dot(
        chosen, dig_in[...].reshape(span, half_width),
        precision=lax.Precision.HIGHEST, preferred_element_type=jnp.float32,
    )
    dig_mine[:, :half_width] = ordered[:blocks]
    dig_mine[:, half_width:] = ordered[blocks:]
    exchange = pltpu.make_async_remote_copy(
        src_ref=dig_mine, dst_ref=dig_theirs, send_sem=e_sem.at[0], recv_sem=e_sem.at[1],
        device_id=other_replica, device_id_type=MESH,
    )
    exchange.start()

    def drain_digest(step, carry):
        d_copy((me + step) % count).wait_send()
        return carry

    lax.fori_loop(1, count, drain_digest, 0)
    for m in range(planes):
        for half in halves(m):
            def drain_spot(j, carry, m=m, half=half):
                x_copy(target_of(m, j), half).wait_send()
                return carry

            def drain_part(j, carry, m=m, half=half):
                p_copy(partner(m), (spot + group - j) % group, half).wait_send()
                return carry

            lax.fori_loop(1, group + (m > 0), drain_spot, 0)
            lax.fori_loop(1, group, drain_part, 0)

    digest_ref[pl.ds(pl.multiple_of(side * blocks, blocks), blocks), :] = dig_mine[...]
    exchange.wait()
    digest_ref[pl.ds(pl.multiple_of((1 - side) * blocks, blocks), blocks), :] = dig_theirs[...]

    summed = total[0]
    for m in range(1, planes, 2):
        z_copy(m).wait_recv()
        summed += plane_in[m].astype(jnp.float32)
    gate_sum = summed[:, :width] * scale
    up_sum = summed[:, width:] * scale
    hidden_ref[...] = (gate_sum / (1.0 + jnp.exp(-gate_sum)) * up_sum).astype(jnp.bfloat16)

    for m in range(1, planes):
        for half in halves(m):
            z_copy(m, half).wait_send()


def on_device(trainer_gate, trainer_up, owner_map, sketch_seeds, probes):
    local_rows, _, slice_width = trainer_gate.shape
    count = lax.axis_size("fsdp")
    ranks = min(16, count)
    subgroups = count // ranks
    width = slice_width // ranks
    narrow = width // subgroups
    group = 4
    planes = count // group
    total_rows = local_rows * count
    blocks = total_rows // LANES
    nb = local_rows // LANES
    dig_rows = -(-2 * nb // 8) * 8
    rows = probes.shape[2]
    bf16, f32 = jnp.bfloat16, jnp.float32
    dma = pltpu.SemaphoreType.DMA
    digest, hidden = pl.pallas_call(
        functools.partial(kernel, count, group, subgroups, width, blocks),
        out_shape=(
            pltpu.VMEM((2 * blocks, width), f32),
            pltpu.VMEM((rows, width), bf16),
        ),
        in_specs=[pl.BlockSpec(memory_space=pl.ANY)] * 5,
        out_specs=[pl.BlockSpec(memory_space=pltpu.VMEM)] * 2,
        scratch_shapes=[
            pltpu.SMEM((blocks,), jnp.int32),
            pltpu.VMEM((blocks, LANES), jnp.int32),
            pltpu.VMEM((rows, total_rows), bf16),
            pltpu.VMEM((blocks, rows, LANES), bf16),
            pltpu.VMEM((local_rows, slice_width), bf16),
            pltpu.VMEM((local_rows, slice_width), bf16),
            pltpu.VMEM((count, rows, local_rows), bf16),
            pltpu.VMEM((count, rows, local_rows), bf16),
            pltpu.VMEM((count, rows, 2 * width), bf16),
            pltpu.VMEM((count, rows, 2 * width), bf16),
            pltpu.VMEM((planes, rows, 2 * width), f32),
            pltpu.VMEM((planes, rows, 2 * width), bf16),
            pltpu.VMEM((planes, rows, 2 * width), bf16),
            pltpu.VMEM((ranks, dig_rows, width // 2), f32),
            pltpu.VMEM((count, dig_rows, width // 2), f32),
            pltpu.VMEM((blocks, width), f32),
            pltpu.VMEM((blocks, width), f32),
            dma((4,)), dma((4,)),
            dma((2 * count,)), dma((2 * count,)),
            dma((2 * count,)), dma((2 * count,)),
            dma((2 * planes,)), dma((2 * planes,)),
            dma((count,)), dma((count,)),
            dma((2,)),
        ],
        compiler_params=pltpu.CompilerParams(
            collective_id=0, has_side_effects=True, vmem_limit_bytes=60 * 2**20
        ),
    )(
        probes.reshape(rows, total_rows),
        trainer_gate.reshape(local_rows, slice_width),
        trainer_up.reshape(local_rows, slice_width),
        owner_map,
        sketch_seeds.reshape(blocks, LANES),
    )
    if subgroups > 1:
        member = lax.axis_index("fsdp")
        digest = lax.dynamic_slice_in_dim(digest, (member % subgroups) * narrow, narrow, 1)
    return (
        digest.reshape(2, blocks, 1, narrow),
        hidden.reshape(1, 1, rows, 1, width),
    )


def solution(mesh):
    placed = (P("fsdp", "dp", None), P("fsdp", "dp", None), P(), P(), P("rep", "fsdp", None, None))
    return jax.shard_map(
        on_device,
        mesh=mesh,
        in_specs=placed,
        out_specs=(P(None, None, "dp", "fsdp"), P("rep", "fsdp", None, "dp", None)),
        check_vma=False,
    )
```

```python
import functools

import jax
import jax.numpy as jnp
from jax import lax
from jax.experimental import pallas as pl
from jax.experimental.pallas import tpu as pltpu
from jax.sharding import PartitionSpec as P

MESH = pl.DeviceIdType.MESH
LANES = 128


def kernel(
    count, group, subgroups, width, blocks,
    probes_hbm, gate_hbm, up_hbm, owner_hbm, seeds_hbm,
    digest_ref, hidden_ref,
    owner_ref, seeds_ref, x_flat, x, gate, up, stage, got, part, part_in, total, plane_out, plane_in, dig_out, dig_in, dig_mine, dig_theirs,
    x_load, load_sem, x_send, x_recv, p_send, p_recv, z_send, z_recv, d_send, d_recv, e_sem,
):
    planes = count // group
    rows = x.shape[1]
    local_rows = gate.shape[0]
    nb = local_rows // LANES
    ranks = dig_out.shape[0]
    dig_rows = dig_out.shape[1]
    me = lax.axis_index("fsdp")
    plane, spot = me // group, me % group
    replica = lax.axis_index("rep")
    side = replica % 2
    other_replica = {"rep": replica + 1 - 2 * side}

    def peer(index):
        return {"fsdp": index}

    def remote(src, dst, send, recv, index):
        return pltpu.make_async_remote_copy(
            src_ref=src, dst_ref=dst, send_sem=send, recv_sem=recv,
            device_id=peer(index), device_id_type=MESH,
        )

    barrier = pltpu.get_barrier_semaphore()

    def greet(step, carry):
        pl.semaphore_signal(
            barrier, inc=1, device_id=peer((me + step) % count), device_id_type=MESH
        )
        return carry

    load_owner = pltpu.make_async_copy(owner_hbm, owner_ref, load_sem.at[2])
    load_seeds = pltpu.make_async_copy(seeds_hbm, seeds_ref, load_sem.at[3])
    load_gate = pltpu.make_async_copy(gate_hbm, gate, load_sem.at[0])
    load_up = pltpu.make_async_copy(up_hbm, up, load_sem.at[1])
    quarter = blocks // 4
    loads = []
    for c in range(4):
        columns = pl.ds(c * quarter * LANES, quarter * LANES)
        loads.append(
            pltpu.make_async_copy(probes_hbm.at[:, columns], x_flat.at[:, columns], x_load.at[c])
        )
    load_owner.start()
    for load in loads:
        load.start()
    lax.fori_loop(1, count, greet, 0)
    pl.semaphore_signal(barrier, inc=1, device_id=other_replica, device_id_type=MESH)
    load_gate.start()
    load_up.start()
    load_seeds.start()
    for c in range(4):
        loads[c].wait()
        for block in range(c * quarter, (c + 1) * quarter):
            x[block] = x_flat[:, block * LANES : (block + 1) * LANES]
    load_owner.wait()

    def pick(target, into):
        for i in range(nb):
            block = owner_ref[target * nb + i]
            into[target, :, i * LANES : (i + 1) * LANES] = x[block]


    def rows_of(half):
        return pl.ds(0, rows)

    def slot(index, half):
        return index

    def halves(m):
        return (None,)

    def x_copy(target, half=None):
        return remote(
            stage.at[target, rows_of(half)], got.at[me, rows_of(half)],
            x_send.at[slot(target, half)], x_recv.at[slot(me, half)], target,
        )

    def x_arrival(source, half=None):
        return remote(
            stage.at[source, rows_of(half)], got.at[source, rows_of(half)],
            x_send.at[slot(source, half)], x_recv.at[slot(source, half)], source,
        )

    pl.semaphore_wait(barrier, count)
    def partner(m):
        other = plane * 0
        for bit in range((planes - 1).bit_length()):
            digit = (plane // 2**bit) % 2
            other = other + 2**bit * (1 - digit if (m >> bit) & 1 else digit)
        return other

    def target_of(m, j):
        return partner(m) * group + (spot + j) % group

    def send(m, j, half=None):
        if half != 1:
            pick(target_of(m, j), stage)
        x_copy(target_of(m, j), half).start()

    def send_phase(m, last, half=None):
        def one(j, carry):
            send(m, j, half)
            return carry

        lax.fori_loop(1, last, one, 0)

    send_phase(2, group + 1)
    send_phase(0, group)
    send_phase(1, group + 1)

    send_phase(3, group + 1)

    pick(me, got)

    def squares(block, acc):
        wide = x[block].astype(jnp.float32)
        return acc + wide * wide

    acc = lax.fori_loop(0, blocks, squares, jnp.zeros((rows, LANES), jnp.float32))
    meansq = jnp.sum(acc, axis=1, keepdims=True) / (blocks * LANES)
    scale = 1.0 / jnp.sqrt(meansq + 1e-05)

    load_seeds.wait()
    row_id = lax.broadcasted_iota(jnp.int32, (16, LANES), 0)
    for_left, for_right = [], []
    for i in range(nb):
        held = lax.broadcasted_iota(jnp.int32, seeds_ref.shape, 0) == owner_ref[me * nb + i]
        seeds = jnp.sum(jnp.where(held, seeds_ref[...], 0), axis=0, keepdims=True)
        signs = jnp.broadcast_to(8 * (1 - 2 * seeds), (16, LANES)).astype(jnp.float32)
        for_left.append(jnp.where(row_id == i, signs, 0.0))
        for_right.append(jnp.where(row_id == nb + i, signs, 0.0))
    for_left = jnp.concatenate(for_left, axis=1).astype(jnp.bfloat16)
    for_right = jnp.concatenate(for_right, axis=1).astype(jnp.bfloat16)
    load_gate.wait()
    load_up.wait()

    def columns_of(t):
        return pl.ds(pl.multiple_of(t * width, width), width)

    half_width = width // 2

    def sketch_all(weights):
        def sketch(t, carry):
            left = pl.ds(pl.multiple_of(t * width, width), half_width)
            right = pl.ds(pl.multiple_of(t * width + half_width, half_width), half_width)
            both = jnp.dot(for_left, weights[:, left], preferred_element_type=jnp.float32)
            both += jnp.dot(for_right, weights[:, right], preferred_element_type=jnp.float32)
            dig_out[t] = both[:dig_rows]
            return carry

        lax.fori_loop(0, ranks, sketch, 0)

    @pl.when(side == 0)
    def _():
        sketch_all(gate)

    @pl.when(side == 1)
    def _():
        sketch_all(up)

    dig_in[me] = dig_out[me // subgroups]

    def d_copy(target):
        return remote(
            dig_out.at[target // subgroups], dig_in.at[me], d_send.at[target], d_recv.at[me], target
        )

    def d_arrival(source):
        return remote(
            dig_out.at[source // subgroups], dig_in.at[source], d_send.at[source],
            d_recv.at[source], source,
        )

    def send_digest(step, carry):
        d_copy((me + step) % count).start()
        return carry

    lax.fori_loop(1, count, send_digest, 0)

    def product(source, half=None):
        rows_in = got[source, rows_of(half)]
        columns = columns_of(source // subgroups)
        return (
            jnp.dot(rows_in, gate[:, columns], preferred_element_type=jnp.float32),
            jnp.dot(rows_in, up[:, columns], preferred_element_type=jnp.float32),
        )

    def p_copy(source_plane, spot_to, half=None):
        index, here = source_plane * group + spot_to, source_plane * group + spot
        return remote(
            part.at[index, rows_of(half)], part_in.at[here, rows_of(half)],
            p_send.at[slot(index, half)], p_recv.at[slot(here, half)],
            plane * group + spot_to,
        )

    def p_arrival(source_plane, spot_from, half=None):
        index = source_plane * group + spot_from
        return remote(
            part.at[index, rows_of(half)], part_in.at[index, rows_of(half)],
            p_send.at[slot(index, half)], p_recv.at[slot(index, half)],
            plane * group + spot_from,
        )

    def z_copy(m, half=None):
        index = m + planes if half == 1 else m
        return remote(
            plane_out.at[m, rows_of(half)], plane_in.at[m, rows_of(half)],
            z_send.at[index], z_recv.at[index],
            partner(m if m % 2 else 1) * group + spot,
        )

    def multiply_other(m, spot_from, half=None):
        source = partner(m) * group + spot_from
        a, b = product(source, half)
        part[source, rows_of(half), :width] = a.astype(jnp.bfloat16)
        part[source, rows_of(half), width:] = b.astype(jnp.bfloat16)
        p_copy(partner(m), spot_from, half).start()

    def multiply_own(m, half=None):
        a, b = product(partner(m) * group + spot, half)
        total[m, rows_of(half), :width] = a
        total[m, rows_of(half), width:] = b

    def start_following(m, j):
        if m >= 2 and m + 1 < planes:
            if m % 2:
                send(m + 1, j)
                return
            if m == 2:
                return

            @pl.when((j - 1) // 2 == spot % 2)
            def _():
                send(m + 1, 2 * ((j - 1) % 2) + 1)
                send(m + 1, 2 * ((j - 1) % 2) + 2)

    def multiply(m):
        def others(j, carry):
            spot_from = (spot + group - j) % group
            x_arrival(partner(m) * group + spot_from).wait_recv()
            start_following(m, j)
            multiply_other(m, spot_from)
            return carry

        lax.fori_loop(1, group, others, 0)
        if m != 0:
            x_arrival(partner(m) * group + spot).wait_recv()
            start_following(m, group)
        multiply_own(m)

    def multiply_staggered(m):
        for odd in range(2):
            for half in halves(m):
                def one(step, carry, odd=odd, half=half):
                    j = 2 - (spot + odd) % 2 + 2 * step
                    spot_from = (spot + group - j) % group
                    x_arrival(partner(m) * group + spot_from, half).wait_recv()
                    start_following(m, 2 * odd + step + 1)

                    @pl.when(j == group)
                    def _():
                        multiply_own(m, half)

                    @pl.when(j != group)
                    def _():
                        multiply_other(m, spot_from, half)

                    return carry

                lax.fori_loop(0, 2, one, 0)

                @pl.when(spot % 2 == odd)
                def _():
                    reduce(m, half)

    def reduce(m, half=None):
        summed = total[m, rows_of(half)]
        if m > 2 and m % 2:
            z_copy(m - 1).wait_recv()
            summed += plane_in[m - 1, rows_of(half)].astype(jnp.float32)
        for j in range(1, group):
            p_arrival(partner(m), (spot + group - j) % group, half).wait_recv()
        for j in range(1, group):
            index = partner(m) * group + (spot + group - j) % group
            summed += part_in[index, rows_of(half)].astype(jnp.float32)
        if m > 0:
            plane_out[m, rows_of(half)] = summed.astype(jnp.bfloat16)
            z_copy(m, half).start()
        else:
            total[m] = summed

    multiply(0)
    multiply(2)
    reduce(0)
    multiply(1)
    reduce(2)
    reduce(1)
    for m in range(3, planes):
        if m % 2:
            multiply_staggered(m)
        else:
            multiply(m)
            reduce(m)

    def wait_digest(step, carry):
        d_arrival((me + step) % count).wait_recv()
        return carry

    lax.fori_loop(1, count, wait_digest, 0)
    span = count * dig_rows
    column = lax.broadcasted_iota(jnp.int32, (8, span), 1)
    inner = column % dig_rows
    place = jnp.where(inner < 2 * nb, (column // dig_rows) * nb + inner % nb, -1)
    owners = jnp.full((8, span), -1, jnp.int32)
    for j in range(blocks):
        owners = jnp.where(place == j, owner_ref[j], owners)
    owners = owners + jnp.where(inner >= nb, blocks, 0)
    owners = jnp.where(inner < 2 * nb, owners, -1)
    wanted = lax.broadcasted_iota(jnp.int32, (2 * blocks, span), 0)
    chosen = jnp.where(jnp.broadcast_to(owners[:1], (2 * blocks, span)) == wanted, 1.0, 0.0)
    ordered = jnp.dot(
        chosen, dig_in[...].reshape(span, half_width),
        precision=lax.Precision.HIGHEST, preferred_element_type=jnp.float32,
    )
    dig_mine[:, :half_width] = ordered[:blocks]
    dig_mine[:, half_width:] = ordered[blocks:]
    exchange = pltpu.make_async_remote_copy(
        src_ref=dig_mine, dst_ref=dig_theirs, send_sem=e_sem.at[0], recv_sem=e_sem.at[1],
        device_id=other_replica, device_id_type=MESH,
    )
    exchange.start()

    def drain_digest(step, carry):
        d_copy((me + step) % count).wait_send()
        return carry

    lax.fori_loop(1, count, drain_digest, 0)
    for m in range(planes):
        for half in halves(m):
            def drain_spot(j, carry, m=m, half=half):
                x_copy(target_of(m, j), half).wait_send()
                return carry

            def drain_part(j, carry, m=m, half=half):
                p_copy(partner(m), (spot + group - j) % group, half).wait_send()
                return carry

            lax.fori_loop(1, group + (m > 0), drain_spot, 0)
            lax.fori_loop(1, group, drain_part, 0)

    digest_ref[pl.ds(pl.multiple_of(side * blocks, blocks), blocks), :] = dig_mine[...]
    exchange.wait()
    digest_ref[pl.ds(pl.multiple_of((1 - side) * blocks, blocks), blocks), :] = dig_theirs[...]

    summed = total[0]
    for m in range(1, planes, 2):
        z_copy(m).wait_recv()
        summed += plane_in[m].astype(jnp.float32)
    gate_sum = summed[:, :width] * scale
    up_sum = summed[:, width:] * scale
    hidden_ref[...] = (gate_sum / (1.0 + jnp.exp(-gate_sum)) * up_sum).astype(jnp.bfloat16)

    for m in range(1, planes):
        for half in halves(m):
            z_copy(m, half).wait_send()


def on_device(trainer_gate, trainer_up, owner_map, sketch_seeds, probes):
    local_rows, _, slice_width = trainer_gate.shape
    count = lax.axis_size("fsdp")
    ranks = min(16, count)
    subgroups = count // ranks
    width = slice_width // ranks
    narrow = width // subgroups
    group = 4
    planes = count // group
    total_rows = local_rows * count
    blocks = total_rows // LANES
    nb = local_rows // LANES
    dig_rows = -(-2 * nb // 8) * 8
    rows = probes.shape[2]
    bf16, f32 = jnp.bfloat16, jnp.float32
    dma = pltpu.SemaphoreType.DMA
    digest, hidden = pl.pallas_call(
        functools.partial(kernel, count, group, subgroups, width, blocks),
        out_shape=(
            pltpu.VMEM((2 * blocks, width), f32),
            pltpu.VMEM((rows, width), bf16),
        ),
        in_specs=[pl.BlockSpec(memory_space=pl.ANY)] * 5,
        out_specs=[pl.BlockSpec(memory_space=pltpu.VMEM)] * 2,
        scratch_shapes=[
            pltpu.SMEM((blocks,), jnp.int32),
            pltpu.VMEM((blocks, LANES), jnp.int32),
            pltpu.VMEM((rows, total_rows), bf16),
            pltpu.VMEM((blocks, rows, LANES), bf16),
            pltpu.VMEM((local_rows, slice_width), bf16),
            pltpu.VMEM((local_rows, slice_width), bf16),
            pltpu.VMEM((count, rows, local_rows), bf16),
            pltpu.VMEM((count, rows, local_rows), bf16),
            pltpu.VMEM((count, rows, 2 * width), bf16),
            pltpu.VMEM((count, rows, 2 * width), bf16),
            pltpu.VMEM((planes, rows, 2 * width), f32),
            pltpu.VMEM((planes, rows, 2 * width), bf16),
            pltpu.VMEM((planes, rows, 2 * width), bf16),
            pltpu.VMEM((ranks, dig_rows, width // 2), f32),
            pltpu.VMEM((count, dig_rows, width // 2), f32),
            pltpu.VMEM((blocks, width), f32),
            pltpu.VMEM((blocks, width), f32),
            dma((4,)), dma((4,)),
            dma((2 * count,)), dma((2 * count,)),
            dma((2 * count,)), dma((2 * count,)),
            dma((2 * planes,)), dma((2 * planes,)),
            dma((count,)), dma((count,)),
            dma((2,)),
        ],
        compiler_params=pltpu.CompilerParams(
            collective_id=0, has_side_effects=True, vmem_limit_bytes=60 * 2**20
        ),
    )(
        probes.reshape(rows, total_rows),
        trainer_gate.reshape(local_rows, slice_width),
        trainer_up.reshape(local_rows, slice_width),
        owner_map,
        sketch_seeds.reshape(blocks, LANES),
    )
    if subgroups > 1:
        member = lax.axis_index("fsdp")
        digest = lax.dynamic_slice_in_dim(digest, (member % subgroups) * narrow, narrow, 1)
    return (
        digest.reshape(2, blocks, 1, narrow),
        hidden.reshape(1, 1, rows, 1, width),
    )


def solution(mesh):
    placed = (P("fsdp", "dp", None), P("fsdp", "dp", None), P(), P(), P("rep", "fsdp", None, None))
    return jax.shard_map(
        on_device,
        mesh=mesh,
        in_specs=placed,
        out_specs=(P(None, None, "dp", "fsdp"), P("rep", "fsdp", None, "dp", None)),
        check_vma=False,
    )
```
